32 devices in a mesh: groups: 2 (over y), blk: 4 (over z), shell: 2 (over x), sub: 2 (over core).
Axes of the slice: x: 2, y: 2, z: 4, core: 2. Of those that a mesh axis runs over, the one named last changes fastest.
Arguments:
- images: bfloat16 [4096, 2, 8192], P(('groups', 'blk'), None, ('shell', 'sub')), parts along dimension 0, may hold values from -12 to 12
- ctf: bfloat16 [4096, 8192], P(('groups', 'blk'), ('shell', 'sub')), parts along dimension 0, may hold values from -1 to 1
- projections: bfloat16 [32, 2, 8192], P(('groups', 'blk'), None, ('shell', 'sub')), parts along dimension 0, may hold values from -5 to 5
- shifts: int32 [4096, 2], P(('groups', 'blk')), parts along dimension 0, may hold values from -6 to 6
- inv_sigma2: float32 [8192], P(('shell', 'sub')), may hold values from 0.5 to 2
- class_ids: int32 [32], P('groups'), parts along dimension 0, may hold values from 0 to 3
- log_prior: float32 [4], replicated, may hold values from -1.5 to 0
- allowed: int32 [8, 2], P(('groups', 'blk')), parts along dimension 0, may hold values from -1 to 3, as said below
Outputs:
- back_data: float32 [32, 2, 8192], P(('groups', 'blk'), None, ('shell', 'sub')), parts along dimension 0
- back_weight: float32 [32, 8192], P(('groups', 'blk'), ('shell', 'sub')), parts along dimension 0
- best_weight: float32 [4096], P(('groups', 'blk', 'shell', 'sub')), parts along dimension 0
The draws below stay inside these ranges and needn't reach their ends.
There are 2 independent parts, one for each index of `groups`. The reference program is written for one: setup_inputs(seed, part) draws one part's arguments, and reference() takes and returns one part's arrays. A program takes and returns all parts, laid end to end along the dimension named above; an argument that names none is the same for every part. Nothing has to cross between parts.
Inputs may be any that keep to these rules, and one draw needn't show every extreme that they name: `allowed`: row b lists distinct orientation block numbers in its first slots, block b always first, then -1 in the remaining slots; between 1 and 2 blocks are listed, and some row lists 2.
All inputs are finite; a program needn't handle non-finite values.
Results may differ from the reference program's by a relative error of at most 0.0055.
Values may be sent and summed in bfloat16 or wider, within the bound.
No kernel may reach another device: no remote copies, remote signals or barrier semaphores. Data moves between devices by JAX's collectives and lax.ppermute only.
A program may use at most 64 MiB of HBM per device.

```python
import math
import jax
import jax.numpy as jnp
from jax import lax

KMAX = 64
BOX = 360
CLASSES = 4
IMG_DEV = 512
OR_DEV = 4
PIXC = 8192
IMAGES = 2048
ORIENTS = 16
MAXB = 2
N_BLK = 4


def shared_fields(key):
    proj = jnp.clip(jax.random.normal(jax.random.fold_in(key, 101), (ORIENTS, 2, PIXC), jnp.float32), -5.0, 5.0)
    ctf = jax.random.uniform(jax.random.fold_in(key, 102), (IMAGES, PIXC), jnp.float32, -1.0, 1.0)
    shifts = jax.random.randint(jax.random.fold_in(key, 103), (IMAGES, 2), -6, 7, dtype=jnp.int32)
    return (proj, ctf, shifts)


def draw_projections(key, part):
    proj, ctf, shifts = shared_fields(key)
    return proj.astype(jnp.bfloat16)


def draw_ctf(key, part):
    proj, ctf, shifts = shared_fields(key)
    return ctf.astype(jnp.bfloat16)


def draw_shifts(key, part):
    proj, ctf, shifts = shared_fields(key)
    return shifts


def draw_images(key, part):
    key = jax.random.fold_in(key, 4)
    values = jax.random.normal(jax.random.fold_in(key, 3), (IMAGES, 2, PIXC), jnp.float32)
    return jnp.clip(values, -12.0, 12.0).astype(jnp.bfloat16)


def draw_allowed(key, part):
    key = jax.random.fold_in(key, 7)
    blocks = jnp.arange(N_BLK, dtype=jnp.int32)
    raw = jax.random.randint(jax.random.fold_in(key, 1), (N_BLK,), 0, MAXB, dtype=jnp.int32)
    counts = jnp.minimum(MAXB, 3 + raw * raw // MAXB)
    star = jax.random.randint(jax.random.fold_in(key, 2), (), 0, N_BLK, dtype=jnp.int32)
    counts = jnp.where(blocks == star, MAXB, counts)
    ranks = jax.random.randint(jax.random.fold_in(key, 3), (N_BLK, N_BLK), 0, 2 ** 20, dtype=jnp.int32) * N_BLK + blocks[None, :]
    ranks = jnp.where(blocks[:, None] == blocks[None, :], -1, ranks)
    order = jnp.argsort(ranks, axis=1).astype(jnp.int32)
    listed = order[:, :MAXB]
    slots = jnp.arange(MAXB, dtype=jnp.int32)[None, :]
    return jnp.where(slots < counts[:, None], listed, -1).astype(jnp.int32)


def set_ends(array, stream_key, low, high):
    spot = [jax.random.randint(jax.random.fold_in(stream_key, axis), (), 0, length) for axis, length in enumerate(array.shape)]
    widest = array.shape.index(max(array.shape))
    beside = spot[:widest] + [(spot[widest] + 1) % array.shape[widest]] + spot[widest + 1:]
    return array.at[tuple(spot)].set(low).at[tuple(beside)].set(high)


def steps_of(own_key, dims, split, low, high):
    loudness, own = 1.0, jax.random.fold_in(own_key, 6)
    for dim, shards_of in split:
        draws = jnp.exp(jax.random.uniform(jax.random.fold_in(own, dim), (shards_of,), jnp.float32, low / len(split), high / len(split)))
        loudness = loudness * jnp.repeat(draws, dims[dim] // shards_of).reshape([-1 if axis == dim else 1 for axis in range(len(dims))])
    return loudness


def setup_inputs(seed: int = 0, part: int = 0) -> dict:
    splits = jax.random.split(jax.random.key(seed), 9)
    part_keys = jax.random.split(jax.random.fold_in(splits[8], part), 9)
    images = draw_images(jax.random.fold_in(jax.random.fold_in(splits[8], part), 71), part)
    ctf = draw_ctf(jax.random.fold_in(jax.random.fold_in(splits[8], part), 71), part)
    projections = draw_projections(jax.random.fold_in(jax.random.fold_in(splits[8], part), 71), part)
    shifts = draw_shifts(jax.random.fold_in(jax.random.fold_in(splits[8], part), 71), part)
    inv_sigma2 = jnp.clip(jnp.exp(math.log(2.0) - 1.3862944 * jax.random.uniform(splits[4], (PIXC,), jnp.float32) ** steps_of(splits[4], (PIXC,), ((0, 4),), -0.2, 0.2)), 0.5, 2.0)
    class_ids = set_ends(jax.random.randint(part_keys[5], (ORIENTS,), 0, CLASSES), jax.random.fold_in(part_keys[5], 1), 0, CLASSES - 1).astype(jnp.int32)
    log_prior = jnp.clip(jax.random.uniform(splits[6], (CLASSES,), jnp.float32, -1.5, 0.0), -1.5, 0.0)
    allowed = draw_allowed(jax.random.fold_in(jax.random.fold_in(splits[8], part), 71), part)
    return {"images": images, "ctf": ctf, "projections": projections, "shifts": shifts, "inv_sigma2": inv_sigma2, "class_ids": class_ids, "log_prior": log_prior, "allowed": allowed}


def prepare(images, ctf, shifts, inv_sigma2, first_pixel):
    width = images.shape[2]
    pixel = first_pixel + jnp.arange(width, dtype=jnp.int32)
    freq_x = (pixel // (2 * KMAX)).astype(jnp.float32)
    freq_y = (pixel % (2 * KMAX) - KMAX).astype(jnp.float32)
    moves = shifts.astype(jnp.float32)
    theta = 2.0 * math.pi / BOX * (moves[:, 0:1] * freq_x[None, :] + moves[:, 1:2] * freq_y[None, :])
    cosine = jnp.cos(theta)
    sine = jnp.sin(theta)
    real_part = images[:, 0].astype(jnp.float32)
    imag_part = images[:, 1].astype(jnp.float32)
    shifted_real = real_part * cosine + imag_part * sine
    shifted_imag = imag_part * cosine - real_part * sine
    factor = ctf.astype(jnp.float32) * inv_sigma2[None, :]
    weighted = jnp.stack([factor * shifted_real, factor * shifted_imag], axis=1).astype(jnp.bfloat16)
    curvature = (factor * ctf.astype(jnp.float32)).astype(jnp.bfloat16)
    return (weighted, curvature)

def posterior(rows, keep_cols):
    masked = jnp.where(keep_cols[None, :], rows, jnp.float32(-1e+30))
    top = lax.optimization_barrier(jnp.max(masked, axis=1, keepdims=True))
    expo = jnp.exp(masked - top)
    total = lax.optimization_barrier(jnp.sum(expo, axis=1, keepdims=True))
    return ((expo / total).astype(jnp.bfloat16), 1.0 / total[:, 0])

def reference(images, ctf, projections, shifts, inv_sigma2, class_ids, log_prior, allowed):

    def prep_block(pack):
        return prepare(pack[0], pack[1], pack[2], inv_sigma2, jnp.int32(0))
    weighted_blocks, curv_blocks = lax.map(prep_block, (images.reshape(N_BLK, IMG_DEV, 2, PIXC), ctf.reshape(N_BLK, IMG_DEV, PIXC), shifts.reshape(N_BLK, IMG_DEV, 2)))
    flat = weighted_blocks.reshape(IMAGES, 2 * PIXC)
    curvature = curv_blocks.reshape(IMAGES, PIXC)
    proj_wide = projections.astype(jnp.float32)
    power = (proj_wide[:, 0] * proj_wide[:, 0] + proj_wide[:, 1] * proj_wide[:, 1]).astype(jnp.bfloat16)
    cross = jnp.dot(flat, projections.reshape(ORIENTS, 2 * PIXC).T, preferred_element_type=jnp.float32)
    self_term = jnp.dot(curvature, power.T, preferred_element_type=jnp.float32)
    classes = class_ids[:, None] == jnp.arange(CLASSES, dtype=jnp.int32)[None, :]
    prior = lax.optimization_barrier(jnp.sum(jnp.where(classes, log_prior[None, :], jnp.float32(0.0)), axis=1))
    scores = (2.0 * cross - self_term) * (1.0 / math.sqrt(PIXC)) + prior[None, :]
    hits = (allowed[:, :, None] == jnp.arange(N_BLK, dtype=jnp.int32)[None, None, :]).astype(jnp.int32)
    kept = jnp.minimum(lax.optimization_barrier(jnp.sum(hits, axis=1)), 1).astype(jnp.int32)

    def post_block(pack):
        return posterior(pack[0], jnp.repeat(pack[1], OR_DEV) == 1)
    weight_blocks, best_blocks = lax.map(post_block, (scores.reshape(N_BLK, IMG_DEV, ORIENTS), kept))
    weights = weight_blocks.reshape(IMAGES, ORIENTS)
    back_data = jnp.dot(weights.T, flat, preferred_element_type=jnp.float32).reshape(ORIENTS, 2, PIXC)
    back_weight = jnp.dot(weights.T, curvature, preferred_element_type=jnp.float32)
    return (back_data, back_weight, best_blocks.reshape(IMAGES))
```

```python
import functools
import math

import jax
import jax.numpy as jnp
import ml_dtypes
import numpy as np
from jax import lax
from jax.experimental import pallas as pl
from jax.experimental.pallas import tpu as pltpu
from jax.sharding import PartitionSpec as P

KMAX = 64
BOX = 360
CLASSES = 4
PIXC = 8192
ROW = 2 * KMAX
REACH = 8
GROUP = 16
DIRECT = 4
SPLITS = 3


def split_terms(table):
    terms = []
    rest = table.astype(np.float64)
    for _ in range(SPLITS):
        term = rest.astype(ml_dtypes.bfloat16)
        terms.append(term)
        rest = rest - term.astype(np.float64)
    return np.concatenate(terms, axis=0)


@functools.lru_cache(maxsize=None)
def phase_table(pieces, rows):
    shift = np.arange(-REACH, REACH, dtype=np.float64)[:, None]
    unit = 2.0 * math.pi / BOX
    along_y = unit * shift * np.arange(-KMAX, KMAX, dtype=np.float64)[None, :]
    step = np.broadcast_to(unit * shift, along_y.shape)
    half = SPLITS * 2 * REACH
    tables = []
    for piece in range(pieces):
        first = step * (piece * rows)
        left = split_terms(np.concatenate([np.cos(first), np.sin(first), np.cos(step), np.sin(step)], axis=1))
        right = split_terms(np.concatenate([np.cos(along_y), np.sin(along_y)], axis=1))
        table = np.zeros((128, 6 * ROW), ml_dtypes.bfloat16)
        table[:half, : 4 * ROW] = left
        table[64 : 64 + half, 4 * ROW :] = right
        tables.append(table)
    return np.stack(tables)


def prepare_kernel(rows, place_ref, image_ref, ctf_ref, shift_ref, inv_ref, table_ref, out_ref, wide_ref, phase_ref):
    images = ctf_ref.shape[0]
    pix = rows * ROW
    lane = lax.broadcasted_iota(jnp.int32, (images, 128), 1)
    inner = lane & 63
    moves = jnp.where(lane < 64, shift_ref[:, 0:1], shift_ref[:, 1:2]) + REACH
    hit = ((inner & (2 * REACH - 1)) == moves) & (inner < SPLITS * 2 * REACH)
    onehot = jnp.where(hit, 1.0, 0.0).astype(jnp.bfloat16)
    phase_ref[...] = jnp.dot(onehot, table_ref[0], preferred_element_type=jnp.float32)

    def group(g, carry):
        start = pl.multiple_of(g * GROUP, GROUP)
        slab = pl.multiple_of(g * (GROUP * rows * 2), GROUP * rows * 2)
        wide_ref[...] = image_ref[pl.ds(slab, GROUP * rows * 2), :].astype(jnp.float32)
        phase = phase_ref[pl.ds(start, GROUP), :]
        cos_a, sin_a, cos_s, sin_s, cos_b, sin_b = (phase[:, k * ROW : (k + 1) * ROW] for k in range(6))
        cos_0 = cos_a * cos_b - sin_a * sin_b
        sin_0 = sin_a * cos_b + cos_a * sin_b
        cos_1 = cos_0 * cos_s - sin_0 * sin_s
        sin_1 = sin_0 * cos_s + cos_0 * sin_s
        twice = 2.0 * cos_s
        for t in range(rows):
            lanes = slice(t * ROW, (t + 1) * ROW)
            real = wide_ref[pl.ds(2 * t, GROUP, stride=2 * rows), :]
            imag = wide_ref[pl.ds(2 * t + 1, GROUP, stride=2 * rows), :]
            ctf = ctf_ref[pl.ds(start, GROUP), lanes].astype(jnp.float32)
            factor = ctf * inv_ref[0:1, lanes]
            out_ref[pl.ds(start, GROUP), lanes] = (factor * (real * cos_0 + imag * sin_0)).astype(jnp.bfloat16)
            out_ref[pl.ds(start, GROUP), pl.ds(pix + t * ROW, ROW)] = (
                factor * (imag * cos_0 - real * sin_0)
            ).astype(jnp.bfloat16)
            out_ref[pl.ds(start, GROUP), pl.ds(2 * pix + t * ROW, ROW)] = (factor * ctf).astype(jnp.bfloat16)
            cos_0, cos_1 = cos_1, twice * cos_1 - cos_0
            sin_0, sin_1 = sin_1, twice * sin_1 - sin_0
        return carry

    lax.fori_loop(0, images // GROUP, group, 0)


def prepare(images, ctf, shifts, inv_sigma2, place, pieces):
    count, _, pix = images.shape
    rows = pix // ROW
    step = min(count, 64)
    flat = images.reshape(count, 2, rows, ROW).transpose(0, 2, 1, 3).reshape(count * rows * 2, ROW)
    return pl.pallas_call(
        functools.partial(prepare_kernel, rows),
        grid_spec=pltpu.PrefetchScalarGridSpec(
            num_scalar_prefetch=1,
            grid=(count // step,),
            in_specs=[
                pl.BlockSpec((step * rows * 2, ROW), lambda i, place: (i, 0)),
                pl.BlockSpec((step, pix), lambda i, place: (i, 0)),
                pl.BlockSpec((step, 2), lambda i, place: (i, 0)),
                pl.BlockSpec((1, pix), lambda i, place: (0, 0)),
                pl.BlockSpec((1, 128, 6 * ROW), lambda i, place: (place[0], 0, 0)),
            ],
            out_specs=pl.BlockSpec((step, 3 * pix), lambda i, place: (i, 0)),
            scratch_shapes=[
                pltpu.VMEM((GROUP * rows * 2, ROW), jnp.float32),
                pltpu.VMEM((step, 6 * ROW), jnp.float32),
            ],
        ),
        out_shape=jax.ShapeDtypeStruct((count, 3 * pix), jnp.bfloat16),
        compiler_params=pltpu.CompilerParams(vmem_limit_bytes=16 * 2**20),
        name="prepare",
    )(place.reshape(1), flat, ctf, shifts, inv_sigma2.reshape(1, pix), phase_table(pieces, rows))


def score_kernel(data_ref, *refs):
    *proj_refs, out_ref = refs
    pix = data_ref.shape[1] // 3
    parts = []
    for ref in proj_refs:
        wide = ref[...].astype(jnp.float32)
        real, imag = wide[:, 0, :], wide[:, 1, :]
        parts.append(jnp.concatenate([2.0 * real, 2.0 * imag, -(real * real + imag * imag)], axis=1))
    joint = jnp.concatenate(parts, axis=0).astype(jnp.bfloat16)
    out_ref[...] = lax.dot_general(
        joint, data_ref[...], (((1,), (1,)), ((), ())), preferred_element_type=jnp.float32
    )


def score(data, pieces):
    orients = sum(piece.shape[0] for piece in pieces)
    return pl.pallas_call(
        score_kernel,
        out_shape=jax.ShapeDtypeStruct((orients, data.shape[0]), jnp.float32),
        compiler_params=pltpu.CompilerParams(vmem_limit_bytes=24 * 2**20),
        name="score",
    )(data, *pieces)


def back_kernel(place_ref, one_ref, two_ref, prior_ref, keep_ref, data_ref, best_ref, own_ref, *away_refs):
    share = best_ref.shape[0]
    rows = (one_ref[...] + two_ref[...]) * (1.0 / math.sqrt(PIXC)) + prior_ref[...]
    masked = jnp.where(keep_ref[...] == 1, rows, jnp.float32(-1e30))
    expo = jnp.exp(masked - jnp.max(masked, axis=0, keepdims=True))
    inverse = 1.0 / jnp.sum(expo, axis=0, keepdims=True)
    weights = (expo * inverse).astype(jnp.bfloat16)
    best = inverse[0, 0:share]
    for piece in range(1, one_ref.shape[1] // share):
        best = jnp.where(place_ref[0] == piece, inverse[0, piece * share : (piece + 1) * share], best)
    best_ref[...] = best
    sums = jnp.dot(weights, data_ref[...], preferred_element_type=jnp.float32)
    each = own_ref.shape[0]
    own_ref[...] = sums[0:each]
    for k, ref in enumerate(away_refs):
        ref[...] = sums[(k + 1) * each : (k + 2) * each].astype(ref.dtype)


def back(place, one, two, prior, keep, data, away, pieces):
    orients, count = one.shape
    each = orients // (away + 1)
    wide = data.shape[1]
    vmem = pl.BlockSpec(memory_space=pltpu.VMEM)
    return pl.pallas_call(
        back_kernel,
        in_specs=[pl.BlockSpec(memory_space=pltpu.SMEM)] + [vmem] * 5,
        out_shape=[
            jax.ShapeDtypeStruct((count // pieces,), jnp.float32),
            jax.ShapeDtypeStruct((each, wide), jnp.float32),
        ]
        + [jax.ShapeDtypeStruct((each, wide), jnp.bfloat16)] * away,
        compiler_params=pltpu.CompilerParams(vmem_limit_bytes=32 * 2**20),
        name="back",
    )(place.reshape(1), one, two, prior, keep, data)


def finish_kernel(own_ref, *refs):
    *away_refs, data_ref, weight_ref = refs
    pix = weight_ref.shape[1]
    total = own_ref[...]
    for ref in away_refs:
        total = total + ref[...].astype(jnp.float32)
    data_ref[:, 0, :] = total[:, :pix]
    data_ref[:, 1, :] = total[:, pix : 2 * pix]
    weight_ref[...] = total[:, 2 * pix :]


def finish(own, away):
    each, wide = own.shape
    return pl.pallas_call(
        finish_kernel,
        out_shape=[
            jax.ShapeDtypeStruct((each, 2, wide // 3), jnp.float32),
            jax.ShapeDtypeStruct((each, wide // 3), jnp.float32),
        ],
        compiler_params=pltpu.CompilerParams(vmem_limit_bytes=16 * 2**20),
        name="finish",
    )(own, *away)


def rotate(value, axis, size, by):
    return lax.ppermute(value, axis, [((j + by) % size, j) for j in range(size)])


def body(images, ctf, projections, shifts, inv_sigma2, class_ids, log_prior, allowed):
    count, _, pix = images.shape
    each = projections.shape[0]
    blocks = lax.axis_size("blk")
    pieces = lax.axis_size(("shell", "sub"))
    place = lax.axis_index(("shell", "sub"))
    me = lax.axis_index("blk")

    direct = blocks <= DIRECT
    if direct:
        projs = [projections] + [rotate(projections, "blk", blocks, k) for k in range(1, blocks)]
    else:
        projs = [jnp.roll(lax.all_gather(projections, "blk", axis=0, tiled=True), -me * each, axis=0)]
    data = prepare(images, ctf, shifts, inv_sigma2, place, pieces)

    order = (me + jnp.arange(blocks, dtype=jnp.int32)) % blocks
    listed = jnp.any(allowed[0][:, None] == order[None, :], axis=0).astype(jnp.int32)
    keep = jnp.repeat(listed, each)[:, None]
    classes = class_ids[:, None] == jnp.arange(CLASSES, dtype=jnp.int32)[None, :]
    prior = jnp.sum(jnp.where(classes, log_prior[None, :], jnp.float32(0.0)), axis=1)
    prior = jnp.roll(prior, -me * each)[:, None]

    part = score(data, projs)
    part = part + rotate(part, "sub", 2, 1)
    if lax.axis_size("shell") == 2:
        other = rotate(part, "shell", 2, 1)
    else:
        other = lax.psum(part, "shell") - part
    best, own, *away = back(place, part, other, prior, keep, data, blocks - 1 if direct else 0, pieces)
    if not direct:
        own = lax.psum_scatter(jnp.roll(own, me * each, axis=0), "blk", scatter_dimension=0, tiled=True)
    arrived = [rotate(block, "blk", blocks, blocks - k) for k, block in enumerate(away, start=1)]
    back_data, back_weight = finish(own, arrived)
    return (back_data, back_weight, best)


def solution(mesh):
    in_specs = (
        P(("groups", "blk"), None, ("shell", "sub")),
        P(("groups", "blk"), ("shell", "sub")),
        P(("groups", "blk"), None, ("shell", "sub")),
        P(("groups", "blk"), None),
        P(("shell", "sub")),
        P("groups"),
        P(),
        P(("groups", "blk"), None),
    )
    out_specs = (
        P(("groups", "blk"), None, ("shell", "sub")),
        P(("groups", "blk"), ("shell", "sub")),
        P(("groups", "blk", "shell", "sub")),
    )
    return jax.shard_map(body, mesh=mesh, in_specs=in_specs, out_specs=out_specs, check_vma=False)
```

```python
import functools
import math

import jax
import jax.numpy as jnp
import ml_dtypes
import numpy as np
from jax import lax
from jax.experimental import pallas as pl
from jax.experimental.pallas import tpu as pltpu
from jax.sharding import PartitionSpec as P

KMAX = 64
BOX = 360
CLASSES = 4
PIXC = 8192
ROW = 2 * KMAX
REACH = 8
GROUP = 16
DIRECT = 4
SPLITS = 3


def split_terms(table):
    terms = []
    rest = table.astype(np.float64)
    for _ in range(SPLITS):
        term = rest.astype(ml_dtypes.bfloat16)
        terms.append(term)
        rest = rest - term.astype(np.float64)
    return np.concatenate(terms, axis=0)


@functools.lru_cache(maxsize=None)
def phase_table(pieces, rows):
    shift = np.arange(-REACH, REACH, dtype=np.float64)[:, None]
    unit = 2.0 * math.pi / BOX
    along_y = unit * shift * np.arange(-KMAX, KMAX, dtype=np.float64)[None, :]
    step = np.broadcast_to(unit * shift, along_y.shape)
    half = SPLITS * 2 * REACH
    tables = []
    for piece in range(pieces):
        first = step * (piece * rows)
        left = split_terms(np.concatenate([np.cos(first), np.sin(first), np.cos(step), np.sin(step)], axis=1))
        right = split_terms(np.concatenate([np.cos(along_y), np.sin(along_y)], axis=1))
        table = np.zeros((128, 6 * ROW), ml_dtypes.bfloat16)
        table[:half, : 4 * ROW] = left
        table[64 : 64 + half, 4 * ROW :] = right
        tables.append(table)
    return np.stack(tables)


@functools.lru_cache(maxsize=None)
def spread_table(rows):
    table = np.zeros((2, rows, 8, 8, rows, 2), ml_dtypes.bfloat16)
    for image in range(8):
        for row in range(rows):
            for part in range(2):
                table[part, row, image, image, row, part] = 1
    return table.reshape(16 * rows, 16 * rows)


def prepare_kernel(
    rows,
    image_hbm,
    ctf_hbm,
    shift_hbm,
    inv_hbm,
    table_hbm,
    spread_hbm,
    out_ref,
    image_ref,
    ctf_ref,
    shift_ref,
    inv_ref,
    table_ref,
    spread_ref,
    phase_ref,
    even_ref,
    odd_ref,
    chunk_sems,
    sems,
):
    images = ctf_ref.shape[0]
    pix = rows * ROW
    chunks = chunk_sems.shape[1]
    each = images // chunks
    lines = 2 * rows
    half = 8 * lines
    place = lax.axis_index(("shell", "sub"))

    def chunk_copies(c):
        image_rows = pl.ds(c * each * lines, each * lines)
        ctf_rows = pl.ds(c * each, each)
        return (
            pltpu.make_async_copy(image_hbm.at[image_rows], image_ref.at[image_rows], chunk_sems.at[0, c]),
            pltpu.make_async_copy(ctf_hbm.at[ctf_rows], ctf_ref.at[ctf_rows], chunk_sems.at[1, c]),
        )

    first = (
        pltpu.make_async_copy(shift_hbm, shift_ref, sems.at[0]),
        pltpu.make_async_copy(table_hbm.at[place], table_ref, sems.at[1]),
    )
    second = (
        pltpu.make_async_copy(spread_hbm, spread_ref, sems.at[2]),
        pltpu.make_async_copy(inv_hbm, inv_ref, sems.at[3]),
    )
    for copy in first + second:
        copy.start()
    for c in range(chunks):
        for copy in chunk_copies(c):
            copy.start()

    for copy in first:
        copy.wait()
    line = lax.broadcasted_iota(jnp.int32, (128, images), 0)
    inner = line & 63
    moves = jnp.where(line < 64, shift_ref[0:1, :], shift_ref[1:2, :]) + REACH
    hit = ((inner & (2 * REACH - 1)) == moves) & (inner < SPLITS * 2 * REACH)
    phase_ref[...] = lax.dot_general(
        jnp.where(hit, 1.0, 0.0).astype(jnp.bfloat16),
        table_ref[...],
        (((0,), (0,)), ((), ())),
        preferred_element_type=jnp.float32,
    )
    for copy in second:
        copy.wait()

    def spread(g, ref):
        slab = pl.multiple_of(g * (2 * half), 2 * half)
        pair = jnp.concatenate([image_ref[pl.ds(slab, half), :], image_ref[pl.ds(slab + half, half), :]], axis=1)
        ref[...] = jnp.dot(spread_ref[...], pair, preferred_element_type=jnp.float32)

    def weigh(g, ref):
        start = pl.multiple_of(g * GROUP, GROUP)
        phase = phase_ref[pl.ds(start, GROUP), :]
        cos_a, sin_a, cos_s, sin_s, cos_b, sin_b = (phase[:, k * ROW : (k + 1) * ROW] for k in range(6))
        cos_0 = cos_a * cos_b - sin_a * sin_b
        sin_0 = sin_a * cos_b + cos_a * sin_b
        cos_1 = cos_0 * cos_s - sin_0 * sin_s
        sin_1 = sin_0 * cos_s + cos_0 * sin_s
        twice = 2.0 * cos_s
        for t in range(rows):
            lanes = slice(t * ROW, (t + 1) * ROW)
            a, b = 8 * t, 8 * (rows + t)
            real = jnp.concatenate([ref[a : a + 8, :ROW], ref[a : a + 8, ROW:]], axis=0)
            imag = jnp.concatenate([ref[b : b + 8, :ROW], ref[b : b + 8, ROW:]], axis=0)
            ctf = ctf_ref[pl.ds(start, GROUP), lanes].astype(jnp.float32)
            factor = ctf * inv_ref[0:1, lanes]
            out_ref[pl.ds(start, GROUP), lanes] = (factor * (real * cos_0 + imag * sin_0)).astype(jnp.bfloat16)
            out_ref[pl.ds(start, GROUP), pl.ds(pix + t * ROW, ROW)] = (
                factor * (imag * cos_0 - real * sin_0)
            ).astype(jnp.bfloat16)
            out_ref[pl.ds(start, GROUP), pl.ds(2 * pix + t * ROW, ROW)] = (factor * ctf).astype(jnp.bfloat16)
            cos_0, cos_1 = cos_1, twice * cos_1 - cos_0
            sin_0, sin_1 = sin_1, twice * sin_1 - sin_0

    groups = images // GROUP
    pairs = groups // chunks // 2
    for copy in chunk_copies(0):
        copy.wait()
    spread(0, even_ref)
    for c in range(chunks):
        if c + 1 < chunks:
            for copy in chunk_copies(c + 1):
                copy.wait()

        def step(i, carry):
            g = 2 * (c * pairs + i)
            spread(g + 1, odd_ref)
            weigh(g, even_ref)
            spread(jnp.minimum(g + 2, groups - 1), even_ref)
            weigh(g + 1, odd_ref)
            return carry

        lax.fori_loop(0, pairs, step, 0)


def in_hbm(value):
    return pltpu.with_memory_space_constraint(value, pltpu.HBM)


def prepare(images, ctf, shifts, inv_sigma2, pieces):
    count, _, pix = images.shape
    rows = pix // ROW
    chunks = max(1, min(8, count // (2 * GROUP)))
    flat = images.reshape(count, 2, rows, ROW).transpose(0, 2, 1, 3).reshape(count * rows * 2, ROW)
    args = (flat, ctf, shifts.T, inv_sigma2.reshape(1, pix), phase_table(pieces, rows), spread_table(rows))
    return pl.pallas_call(
        functools.partial(prepare_kernel, rows),
        in_specs=[pl.BlockSpec(memory_space=pltpu.HBM)] * len(args),
        out_specs=pl.BlockSpec(memory_space=pltpu.VMEM),
        out_shape=pltpu.VMEM((count, 3 * pix), jnp.bfloat16),
        scratch_shapes=[
            pltpu.VMEM(flat.shape, jnp.bfloat16),
            pltpu.VMEM(ctf.shape, jnp.bfloat16),
            pltpu.VMEM((2, count), jnp.int32),
            pltpu.VMEM((1, pix), jnp.float32),
            pltpu.VMEM((128, 6 * ROW), jnp.bfloat16),
            pltpu.VMEM((16 * rows, 16 * rows), jnp.bfloat16),
            pltpu.VMEM((count, 6 * ROW), jnp.float32),
            pltpu.VMEM((16 * rows, 2 * ROW), jnp.float32),
            pltpu.VMEM((16 * rows, 2 * ROW), jnp.float32),
            pltpu.SemaphoreType.DMA((2, chunks)),
            pltpu.SemaphoreType.DMA((4,)),
        ],
        compiler_params=pltpu.CompilerParams(vmem_limit_bytes=24 * 2**20),
        name="prepare",
    )(*[in_hbm(jnp.asarray(arg)) for arg in args])


def score_kernel(blocks, turned, data_ref, allowed_ref, class_ref, prior_ref, *refs):
    *proj_refs, out_ref = refs
    orients = out_ref.shape[0]
    each = orients // blocks
    me = lax.axis_index("blk") if turned else 0

    line = lax.broadcasted_iota(jnp.int32, (orients, orients), 0)
    lane = lax.broadcasted_iota(jnp.int32, (orients, orients), 1)
    block = lax.rem(line // each + me, blocks)
    own = lane == block * each + lax.rem(line, each)
    prior = jnp.zeros((orients, orients), jnp.float32)
    for c in range(CLASSES):
        prior = jnp.where(own & (class_ref[...] == c), prior_ref[0:1, c : c + 1], prior)
    bias = jnp.sum(prior, axis=1, keepdims=True)
    listed = jnp.zeros((orients, 1), jnp.bool_)
    for k in range(allowed_ref.shape[1]):
        listed = listed | (block[:, 0:1] == allowed_ref[0:1, k : k + 1])
    bias = jnp.where(listed, bias, jnp.float32(-1e30))
    bias = jnp.where(lax.axis_index(("shell", "sub")) == 0, bias, 0.0)

    parts = []
    for ref in proj_refs:
        wide = ref[...].astype(jnp.float32)
        real, imag = wide[:, 0, :], wide[:, 1, :]
        parts.append(jnp.concatenate([2.0 * real, 2.0 * imag, -(real * real + imag * imag)], axis=1))
    joint = jnp.concatenate(parts, axis=0).astype(jnp.bfloat16)
    raw = lax.dot_general(joint, data_ref[...], (((1,), (1,)), ((), ())), preferred_element_type=jnp.float32)
    out_ref[...] = raw * (1.0 / math.sqrt(PIXC)) + bias


def score(data, allowed, class_ids, log_prior, projs, blocks, turned):
    orients = class_ids.shape[0]
    return pl.pallas_call(
        functools.partial(score_kernel, blocks, turned),
        out_shape=jax.ShapeDtypeStruct((orients, data.shape[0]), jnp.float32),
        compiler_params=pltpu.CompilerParams(vmem_limit_bytes=24 * 2**20),
        name="score",
    )(data, allowed, class_ids.reshape(1, -1), log_prior.reshape(1, -1), *projs)


def back_kernel(parts, data_ref, *refs):
    part_refs, (best_ref, own_ref, *away_refs) = refs[:parts], refs[parts:]
    share = best_ref.shape[0]
    sums = [ref[...] for ref in part_refs]
    while len(sums) > 1:
        sums = [sums[k] + sums[k + 1] for k in range(0, len(sums), 2)]
    rows = sums[0]
    expo = jnp.exp(rows - jnp.max(rows, axis=0, keepdims=True))
    inverse = 1.0 / jnp.sum(expo, axis=0, keepdims=True)
    weights = (expo * inverse).astype(jnp.bfloat16)
    place = lax.axis_index(("shell", "sub"))
    best = inverse[0, 0:share]
    for piece in range(1, rows.shape[1] // share):
        best = jnp.where(place == piece, inverse[0, piece * share : (piece + 1) * share], best)
    best_ref[...] = best
    back = jnp.dot(weights, data_ref[...], preferred_element_type=jnp.float32)
    each = own_ref.shape[0]
    own_ref[...] = back[0:each]
    for k, ref in enumerate(away_refs):
        ref[...] = back[(k + 1) * each : (k + 2) * each].astype(ref.dtype)


def back(data, parts, away, pieces):
    orients, count = parts[0].shape
    each = orients // (away + 1)
    wide = data.shape[1]
    return pl.pallas_call(
        functools.partial(back_kernel, len(parts)),
        out_shape=[
            jax.ShapeDtypeStruct((count // pieces,), jnp.float32),
            jax.ShapeDtypeStruct((each, wide), jnp.float32),
        ]
        + [jax.ShapeDtypeStruct((each, wide), jnp.bfloat16)] * away,
        compiler_params=pltpu.CompilerParams(vmem_limit_bytes=24 * 2**20),
        name="back",
    )(data, *parts)


def finish_kernel(own_ref, *refs):
    *away_refs, data_ref, weight_ref = refs
    pix = weight_ref.shape[1]
    total = own_ref[...]
    for ref in away_refs:
        total = total + ref[...].astype(jnp.float32)
    data_ref[:, 0, :] = total[:, :pix]
    data_ref[:, 1, :] = total[:, pix : 2 * pix]
    weight_ref[...] = total[:, 2 * pix :]


def finish(own, away):
    each, wide = own.shape
    return pl.pallas_call(
        finish_kernel,
        out_shape=[
            jax.ShapeDtypeStruct((each, 2, wide // 3), jnp.float32),
            jax.ShapeDtypeStruct((each, wide // 3), jnp.float32),
        ],
        compiler_params=pltpu.CompilerParams(vmem_limit_bytes=16 * 2**20),
        name="finish",
    )(own, *away)


def rotate(value, axis, size, by):
    return lax.ppermute(value, axis, [((j + by) % size, j) for j in range(size)])


def swap(value, axes, size, mask):
    return lax.ppermute(value, axes, [(j ^ mask, j) for j in range(size)])


def body(images, ctf, projections, shifts, inv_sigma2, class_ids, log_prior, allowed):
    blocks = lax.axis_size("blk")
    pieces = lax.axis_size(("shell", "sub"))
    direct = blocks <= DIRECT

    if direct:
        projs = [projections] + [rotate(projections, "blk", blocks, k) for k in range(1, blocks)]
    else:
        projs = [lax.all_gather(projections, "blk", axis=0, tiled=True)]
    data = prepare(images, ctf, shifts, inv_sigma2, pieces)
    part = score(data, allowed, class_ids, log_prior, projs, blocks, direct)
    if pieces == 4:
        parts = [part, swap(part, ("shell", "sub"), 4, 1), swap(part, ("shell", "sub"), 4, 2), swap(part, ("shell", "sub"), 4, 3)]
    else:
        parts = [lax.psum(part, ("shell", "sub"))]
    best, own, *away = back(data, parts, blocks - 1 if direct else 0, pieces)
    if not direct:
        own = lax.psum_scatter(own, "blk", scatter_dimension=0, tiled=True)
    arrived = [rotate(block, "blk", blocks, blocks - k) for k, block in enumerate(away, start=1)]
    back_data, back_weight = finish(own, arrived)
    return (back_data, back_weight, best)


def solution(mesh):
    in_specs = (
        P(("groups", "blk"), None, ("shell", "sub")),
        P(("groups", "blk"), ("shell", "sub")),
        P(("groups", "blk"), None, ("shell", "sub")),
        P(("groups", "blk"), None),
        P(("shell", "sub")),
        P("groups"),
        P(),
        P(("groups", "blk"), None),
    )
    out_specs = (
        P(("groups", "blk"), None, ("shell", "sub")),
        P(("groups", "blk"), ("shell", "sub")),
        P(("groups", "blk", "shell", "sub")),
    )
    return jax.shard_map(body, mesh=mesh, in_specs=in_specs, out_specs=out_specs, check_vma=False)
```

```python
import functools
import math

import jax
import jax.numpy as jnp
import ml_dtypes
import numpy as np
from jax import lax
from jax.experimental import pallas as pl
from jax.experimental.pallas import tpu as pltpu
from jax.sharding import PartitionSpec as P

KMAX = 64
BOX = 360
CLASSES = 4
PIXC = 8192
ROW = 2 * KMAX
REACH = 8
GROUP = 16
DIRECT = (2, 4)
SPLITS = 3


def split_terms(table):
    terms = []
    rest = table.astype(np.float64)
    for _ in range(SPLITS):
        term = rest.astype(ml_dtypes.bfloat16)
        terms.append(term)
        rest = rest - term.astype(np.float64)
    return np.concatenate(terms, axis=0)


@functools.lru_cache(maxsize=None)
def phase_table(pieces, rows):
    shift = np.arange(-REACH, REACH, dtype=np.float64)[:, None]
    unit = 2.0 * math.pi / BOX
    along_y = unit * shift * np.arange(-KMAX, KMAX, dtype=np.float64)[None, :]
    step = np.broadcast_to(unit * shift, along_y.shape)
    half = SPLITS * 2 * REACH
    tables = []
    for piece in range(pieces):
        first = step * (piece * rows)
        left = split_terms(np.concatenate([np.cos(first), np.sin(first), np.cos(step), np.sin(step)], axis=1))
        right = split_terms(np.concatenate([np.cos(along_y), np.sin(along_y)], axis=1))
        table = np.zeros((128, 6 * ROW), ml_dtypes.bfloat16)
        table[:half, : 4 * ROW] = left
        table[64 : 64 + half, 4 * ROW :] = right
        tables.append(table)
    return np.stack(tables)


def prepare_kernel(
    rows, image_ref, ctf_ref, shift_ref, inv_ref, table_ref, out_ref, phase_ref, even_ref, odd_ref
):
    images = ctf_ref.shape[0]
    pix = rows * ROW
    lines = 2 * rows

    line = lax.broadcasted_iota(jnp.int32, (128, images), 0)
    inner = line & 63
    moves = jnp.where(line < 64, shift_ref[0:1, :], shift_ref[1:2, :]) + REACH
    hit = ((inner & (2 * REACH - 1)) == moves) & (inner < SPLITS * 2 * REACH)
    phase_ref[...] = lax.dot_general(
        jnp.where(hit, 1.0, 0.0).astype(jnp.bfloat16),
        table_ref[lax.axis_index(("shell", "sub"))],
        (((0,), (0,)), ((), ())),
        preferred_element_type=jnp.float32,
    )

    def spread(g, ref):
        for i in range(GROUP):
            line = pl.multiple_of((g * GROUP + i) * lines, lines)
            wide = image_ref[pl.ds(line, lines), :].astype(jnp.float32)
            for slab in range(lines // 8):
                ref[pl.ds((slab * GROUP + i) * 8, 8), :] = wide[8 * slab : 8 * slab + 8]

    def weigh(g, ref):
        start = pl.multiple_of(g * GROUP, GROUP)
        phase = phase_ref[pl.ds(start, GROUP), :]
        cos_a, sin_a, cos_s, sin_s, cos_b, sin_b = (phase[:, k * ROW : (k + 1) * ROW] for k in range(6))
        cos_0 = cos_a * cos_b - sin_a * sin_b
        sin_0 = sin_a * cos_b + cos_a * sin_b
        cos_1 = cos_0 * cos_s - sin_0 * sin_s
        sin_1 = sin_0 * cos_s + cos_0 * sin_s
        twice = 2.0 * cos_s
        for t in range(rows):
            lanes = slice(t * ROW, (t + 1) * ROW)
            line = 8 * GROUP * (t // 4) + 2 * (t % 4)
            real = ref[pl.ds(line, GROUP, stride=8), :]
            imag = ref[pl.ds(line + 1, GROUP, stride=8), :]
            ctf = ctf_ref[pl.ds(start, GROUP), lanes].astype(jnp.float32)
            factor = ctf * inv_ref[0:1, lanes]
            out_ref[pl.ds(start, GROUP), lanes] = (factor * (real * cos_0 + imag * sin_0)).astype(jnp.bfloat16)
            out_ref[pl.ds(start, GROUP), pl.ds(pix + t * ROW, ROW)] = (
                factor * (imag * cos_0 - real * sin_0)
            ).astype(jnp.bfloat16)
            out_ref[pl.ds(start, GROUP), pl.ds(2 * pix + t * ROW, ROW)] = (factor * ctf).astype(jnp.bfloat16)
            cos_0, cos_1 = cos_1, twice * cos_1 - cos_0
            sin_0, sin_1 = sin_1, twice * sin_1 - sin_0

    def step(i, carry):
        spread(2 * i, even_ref)
        weigh(2 * i, even_ref)
        spread(2 * i + 1, odd_ref)
        weigh(2 * i + 1, odd_ref)
        return carry

    lax.fori_loop(0, images // (2 * GROUP), step, 0)


def prepare(images, ctf, shifts, inv_sigma2, pieces):
    count, _, pix = images.shape
    rows = pix // ROW
    flat = images.reshape(count, 2, rows, ROW).transpose(0, 2, 1, 3).reshape(count * rows * 2, ROW)
    args = (flat, ctf, shifts.T, inv_sigma2.reshape(1, pix), phase_table(pieces, rows))
    return pl.pallas_call(
        functools.partial(prepare_kernel, rows),
        in_specs=[pl.BlockSpec(memory_space=pltpu.VMEM)] * len(args),
        out_specs=pl.BlockSpec(memory_space=pltpu.VMEM),
        out_shape=pltpu.VMEM((count, 3 * pix), jnp.bfloat16),
        scratch_shapes=[
            pltpu.VMEM((count, 6 * ROW), jnp.float32),
            pltpu.VMEM((2 * rows * GROUP, ROW), jnp.float32),
            pltpu.VMEM((2 * rows * GROUP, ROW), jnp.float32),
        ],
        compiler_params=pltpu.CompilerParams(vmem_limit_bytes=8 * 2**20),
        name="prepare",
    )(*[pltpu.with_memory_space_constraint(jnp.asarray(arg), pltpu.VMEM) for arg in args])


def score_kernel(blocks, turned, data_ref, allowed_ref, class_ref, prior_ref, *refs):
    *proj_refs, out_ref = refs
    orients = out_ref.shape[0]
    each = orients // blocks
    me = lax.axis_index("blk") if turned else 0

    line = lax.broadcasted_iota(jnp.int32, (orients, orients), 0)
    lane = lax.broadcasted_iota(jnp.int32, (orients, orients), 1)
    block = lax.rem(line // each + me, blocks)
    own = lane == block * each + lax.rem(line, each)
    prior = jnp.zeros((orients, orients), jnp.float32)
    for c in range(CLASSES):
        prior = jnp.where(own & (class_ref[...] == c), prior_ref[0:1, c : c + 1], prior)
    bias = jnp.sum(prior, axis=1, keepdims=True)
    listed = jnp.zeros((orients, 1), jnp.bool_)
    for k in range(allowed_ref.shape[1]):
        listed = listed | (block[:, 0:1] == allowed_ref[0:1, k : k + 1])
    bias = jnp.where(listed, bias, jnp.float32(-1e30))
    bias = jnp.where(lax.axis_index(("shell", "sub")) == 0, bias, 0.0)

    parts = []
    for ref in proj_refs:
        wide = ref[...].astype(jnp.float32)
        real, imag = wide[:, 0, :], wide[:, 1, :]
        parts.append(jnp.concatenate([2.0 * real, 2.0 * imag, -(real * real + imag * imag)], axis=1))
    joint = jnp.concatenate(parts, axis=0).astype(jnp.bfloat16)
    raw = lax.dot_general(joint, data_ref[...], (((1,), (1,)), ((), ())), preferred_element_type=jnp.float32)
    if turned:
        came = [raw[k * each : (k + 1) * each] for k in range(blocks)]
        leave = came[:1]
        for k in range(1, blocks):
            at = lax.rem(me + k, blocks) ^ me
            value = came[1]
            for other in range(2, blocks):
                value = jnp.where(at == other, came[other], value)
            leave.append(value)
        raw = jnp.concatenate(leave, axis=0)
    out_ref[...] = raw * (1.0 / math.sqrt(PIXC)) + bias


def score(data, allowed, class_ids, log_prior, projs, blocks, turned):
    orients = class_ids.shape[0]
    return pl.pallas_call(
        functools.partial(score_kernel, blocks, turned),
        out_shape=jax.ShapeDtypeStruct((orients, data.shape[0]), jnp.float32),
        compiler_params=pltpu.CompilerParams(vmem_limit_bytes=24 * 2**20),
        name="score",
    )(data, allowed, class_ids.reshape(1, -1), log_prior.reshape(1, -1), *projs)


def back_kernel(parts, data_ref, *refs):
    part_refs, (best_ref, own_ref, *away_refs) = refs[:parts], refs[parts:]
    share = best_ref.shape[0]
    sums = [ref[...] for ref in part_refs]
    while len(sums) > 1:
        sums = [sums[k] + sums[k + 1] for k in range(0, len(sums), 2)]
    rows = sums[0]
    expo = jnp.exp(rows - jnp.max(rows, axis=0, keepdims=True))
    inverse = 1.0 / jnp.sum(expo, axis=0, keepdims=True)
    weights = (expo * inverse).astype(jnp.bfloat16)
    place = lax.axis_index(("shell", "sub"))
    best = inverse[0, 0:share]
    for piece in range(1, rows.shape[1] // share):
        best = jnp.where(place == piece, inverse[0, piece * share : (piece + 1) * share], best)
    best_ref[...] = best
    back = jnp.dot(weights, data_ref[...], preferred_element_type=jnp.float32)
    each = own_ref.shape[0]
    own_ref[...] = back[0:each]
    for k, ref in enumerate(away_refs):
        ref[...] = back[(k + 1) * each : (k + 2) * each].astype(ref.dtype)


def back(data, parts, away, pieces):
    orients, count = parts[0].shape
    each = orients // (away + 1)
    wide = data.shape[1]
    return pl.pallas_call(
        functools.partial(back_kernel, len(parts)),
        out_shape=[
            jax.ShapeDtypeStruct((count // pieces,), jnp.float32),
            jax.ShapeDtypeStruct((each, wide), jnp.float32),
        ]
        + [jax.ShapeDtypeStruct((each, wide), jnp.bfloat16)] * away,
        compiler_params=pltpu.CompilerParams(vmem_limit_bytes=24 * 2**20),
        name="back",
    )(data, *parts)


def finish_kernel(own_ref, *refs):
    *away_refs, data_ref, weight_ref = refs
    pix = weight_ref.shape[1]
    total = own_ref[...]
    for ref in away_refs:
        total = total + ref[...].astype(jnp.float32)
    data_ref[:, 0, :] = total[:, :pix]
    data_ref[:, 1, :] = total[:, pix : 2 * pix]
    weight_ref[...] = total[:, 2 * pix :]


def finish(own, away):
    each, wide = own.shape
    return pl.pallas_call(
        finish_kernel,
        out_shape=[
            jax.ShapeDtypeStruct((each, 2, wide // 3), jnp.float32),
            jax.ShapeDtypeStruct((each, wide // 3), jnp.float32),
        ],
        compiler_params=pltpu.CompilerParams(vmem_limit_bytes=16 * 2**20),
        name="finish",
    )(own, *away)


def opening_kernel(out_ref):
    out_ref[...] = jnp.zeros_like(out_ref)


def opening():
    return pl.pallas_call(
        opening_kernel,
        out_specs=pl.BlockSpec(memory_space=pltpu.VMEM),
        out_shape=pltpu.VMEM((8, 128), jnp.float32),
        compiler_params=pltpu.CompilerParams(vmem_limit_bytes=2**20, has_side_effects=True),
        cost_estimate=pl.CostEstimate(flops=10**10, bytes_accessed=10**7, transcendentals=0),
        name="opening",
    )()


def rotate(value, axis, size, by):
    return lax.ppermute(value, axis, [((j + by) % size, j) for j in range(size)])


def swap(value, axes, size, mask):
    return lax.ppermute(value, axes, [(j ^ mask, j) for j in range(size)])


def body(images, ctf, projections, shifts, inv_sigma2, class_ids, log_prior, allowed):
    blocks = lax.axis_size("blk")
    pieces = lax.axis_size(("shell", "sub"))
    direct = blocks in DIRECT

    first = opening()
    projections, first = lax.optimization_barrier((projections, first))
    if direct:
        projs = [projections] + [swap(projections, "blk", blocks, k) for k in range(1, blocks)]
    else:
        projs = [lax.all_gather(projections, "blk", axis=0, tiled=True)]
    data = prepare(images, ctf, shifts, inv_sigma2, pieces)
    part = score(data, allowed, class_ids, log_prior, projs, blocks, direct)
    if pieces == 4:
        parts = [part, swap(part, ("shell", "sub"), 4, 1), swap(part, ("shell", "sub"), 4, 2), swap(part, ("shell", "sub"), 4, 3)]
    else:
        parts = [lax.psum(part, ("shell", "sub"))]
    best, own, *away = back(data, parts, blocks - 1 if direct else 0, pieces)
    if not direct:
        own = lax.psum_scatter(own, "blk", scatter_dimension=0, tiled=True)
    arrived = [rotate(block, "blk", blocks, blocks - k) for k, block in enumerate(away, start=1)]
    back_data, back_weight = finish(own, arrived)
    return (back_data, back_weight, best)


def solution(mesh):
    in_specs = (
        P(("groups", "blk"), None, ("shell", "sub")),
        P(("groups", "blk"), ("shell", "sub")),
        P(("groups", "blk"), None, ("shell", "sub")),
        P(("groups", "blk"), None),
        P(("shell", "sub")),
        P("groups"),
        P(),
        P(("groups", "blk"), None),
    )
    out_specs = (
        P(("groups", "blk"), None, ("shell", "sub")),
        P(("groups", "blk"), ("shell", "sub")),
        P(("groups", "blk", "shell", "sub")),
    )
    return jax.shard_map(body, mesh=mesh, in_specs=in_specs, out_specs=out_specs, check_vma=False)
```

```python
import functools
import math

import jax
import jax.numpy as jnp
import ml_dtypes
import numpy as np
from jax import lax
from jax.experimental import pallas as pl
from jax.experimental.pallas import tpu as pltpu
from jax.sharding import PartitionSpec as P

KMAX = 64
BOX = 360
CLASSES = 4
PIXC = 8192
ROW = 2 * KMAX
REACH = 8
GROUP = 16
FETCH = {2: (1,), 4: (1, 3, 2)}
RETURN = {2: (1,), 4: (1, 2, 3)}
SHARE = (1, 2, 3)
SPLITS = 3


def split_terms(table):
    terms = []
    rest = table.astype(np.float64)
    for _ in range(SPLITS):
        term = rest.astype(ml_dtypes.bfloat16)
        terms.append(term)
        rest = rest - term.astype(np.float64)
    return np.concatenate(terms, axis=0)


@functools.lru_cache(maxsize=None)
def phase_table(pieces, rows):
    shift = np.arange(-REACH, REACH, dtype=np.float64)[:, None]
    unit = 2.0 * math.pi / BOX
    along_y = unit * shift * np.arange(-KMAX, KMAX, dtype=np.float64)[None, :]
    step = np.broadcast_to(unit * shift, along_y.shape)
    half = SPLITS * 2 * REACH
    tables = []
    for piece in range(pieces):
        first = step * (piece * rows)
        left = split_terms(np.concatenate([np.cos(first), np.sin(first), np.cos(step), np.sin(step)], axis=1))
        right = split_terms(np.concatenate([np.cos(along_y), np.sin(along_y)], axis=1))
        table = np.zeros((128, 6 * ROW), ml_dtypes.bfloat16)
        table[:half, : 4 * ROW] = left
        table[64 : 64 + half, 4 * ROW :] = right
        tables.append(table)
    return np.stack(tables)


def prepare_kernel(
    rows, image_ref, ctf_ref, shift_ref, inv_ref, table_ref, first_ref, out_ref, phase_ref, even_ref, odd_ref
):
    images = ctf_ref.shape[0]
    pix = rows * ROW
    lines = 2 * rows

    line = lax.broadcasted_iota(jnp.int32, (128, images), 0)
    inner = line & 63
    moves = jnp.where(line < 64, shift_ref[0:1, :], shift_ref[1:2, :]) + REACH
    hit = ((inner & (2 * REACH - 1)) == moves) & (inner < SPLITS * 2 * REACH)
    phase_ref[...] = lax.dot_general(
        jnp.where(hit, 1.0, 0.0).astype(jnp.bfloat16),
        table_ref[lax.axis_index(("shell", "sub"))],
        (((0,), (0,)), ((), ())),
        preferred_element_type=jnp.float32,
    )

    def spread(g, ref):
        for i in range(GROUP):
            line = pl.multiple_of((g * GROUP + i) * lines, lines)
            wide = image_ref[pl.ds(line, lines), :].astype(jnp.float32)
            for slab in range(lines // 8):
                ref[pl.ds((slab * GROUP + i) * 8, 8), :] = wide[8 * slab : 8 * slab + 8]

    def weigh(g, ref):
        start = pl.multiple_of(g * GROUP, GROUP)
        phase = phase_ref[pl.ds(start, GROUP), :]
        cos_a, sin_a, cos_s, sin_s, cos_b, sin_b = (phase[:, k * ROW : (k + 1) * ROW] for k in range(6))
        cos_0 = cos_a * cos_b - sin_a * sin_b
        sin_0 = sin_a * cos_b + cos_a * sin_b
        cos_1 = cos_0 * cos_s - sin_0 * sin_s
        sin_1 = sin_0 * cos_s + cos_0 * sin_s
        twice = 2.0 * cos_s
        for t in range(rows):
            lanes = slice(t * ROW, (t + 1) * ROW)
            line = 8 * GROUP * (t // 4) + 2 * (t % 4)
            real = ref[pl.ds(line, GROUP, stride=8), :]
            imag = ref[pl.ds(line + 1, GROUP, stride=8), :]
            ctf = ctf_ref[pl.ds(start, GROUP), lanes].astype(jnp.float32)
            factor = ctf * inv_ref[0:1, lanes]
            out_ref[pl.ds(start, GROUP), lanes] = (factor * (real * cos_0 + imag * sin_0)).astype(jnp.bfloat16)
            out_ref[pl.ds(start, GROUP), pl.ds(pix + t * ROW, ROW)] = (
                factor * (imag * cos_0 - real * sin_0)
            ).astype(jnp.bfloat16)
            out_ref[pl.ds(start, GROUP), pl.ds(2 * pix + t * ROW, ROW)] = (factor * ctf).astype(jnp.bfloat16)
            cos_0, cos_1 = cos_1, twice * cos_1 - cos_0
            sin_0, sin_1 = sin_1, twice * sin_1 - sin_0

    def step(i, carry):
        spread(2 * i, even_ref)
        weigh(2 * i, even_ref)
        spread(2 * i + 1, odd_ref)
        weigh(2 * i + 1, odd_ref)
        return carry

    lax.fori_loop(0, images // (2 * GROUP), step, 0)


def prepare(images, ctf, shifts, inv_sigma2, pieces, first):
    count, _, pix = images.shape
    rows = pix // ROW
    flat = images.reshape(count, 2, rows, ROW).transpose(0, 2, 1, 3).reshape(count * rows * 2, ROW)
    args = (flat, ctf, shifts.T, inv_sigma2.reshape(1, pix), phase_table(pieces, rows), first)
    return pl.pallas_call(
        functools.partial(prepare_kernel, rows),
        in_specs=[pl.BlockSpec(memory_space=pltpu.VMEM)] * len(args),
        out_specs=pl.BlockSpec(memory_space=pltpu.VMEM),
        out_shape=pltpu.VMEM((count, 3 * pix), jnp.bfloat16),
        scratch_shapes=[
            pltpu.VMEM((count, 6 * ROW), jnp.float32),
            pltpu.VMEM((2 * rows * GROUP, ROW), jnp.float32),
            pltpu.VMEM((2 * rows * GROUP, ROW), jnp.float32),
        ],
        compiler_params=pltpu.CompilerParams(vmem_limit_bytes=8 * 2**20),
        name="prepare",
    )(*[pltpu.with_memory_space_constraint(jnp.asarray(arg), pltpu.VMEM) for arg in args])


def score_kernel(blocks, turned, data_ref, allowed_ref, class_ref, prior_ref, *refs):
    *proj_refs, out_ref = refs
    orients = out_ref.shape[0]
    each = orients // blocks
    me = lax.axis_index("blk") if turned else 0

    line = lax.broadcasted_iota(jnp.int32, (orients, orients), 0)
    lane = lax.broadcasted_iota(jnp.int32, (orients, orients), 1)
    block = lax.rem(line // each + me, blocks)
    own = lane == block * each + lax.rem(line, each)
    prior = jnp.zeros((orients, orients), jnp.float32)
    for c in range(CLASSES):
        prior = jnp.where(own & (class_ref[...] == c), prior_ref[0:1, c : c + 1], prior)
    bias = jnp.sum(prior, axis=1, keepdims=True)
    listed = jnp.zeros((orients, 1), jnp.bool_)
    for k in range(allowed_ref.shape[1]):
        listed = listed | (block[:, 0:1] == allowed_ref[0:1, k : k + 1])
    bias = jnp.where(listed, bias, jnp.float32(-1e30))
    bias = jnp.where(lax.axis_index(("shell", "sub")) == 0, bias, 0.0)

    parts = []
    for ref in proj_refs:
        wide = ref[...].astype(jnp.float32)
        real, imag = wide[:, 0, :], wide[:, 1, :]
        parts.append(jnp.concatenate([2.0 * real, 2.0 * imag, -(real * real + imag * imag)], axis=1))
    joint = jnp.concatenate(parts, axis=0).astype(jnp.bfloat16)
    raw = lax.dot_general(joint, data_ref[...], (((1,), (1,)), ((), ())), preferred_element_type=jnp.float32)
    if turned:
        came = [raw[:each]] * blocks
        for k, mask in enumerate(FETCH[blocks], start=1):
            came[mask] = raw[k * each : (k + 1) * each]
        leave = came[:1]
        for k in range(1, blocks):
            at = lax.rem(me + k, blocks) ^ me
            value = came[1]
            for other in range(2, blocks):
                value = jnp.where(at == other, came[other], value)
            leave.append(value)
        raw = jnp.concatenate(leave, axis=0)
    out_ref[...] = raw * (1.0 / math.sqrt(PIXC)) + bias


def score(data, allowed, class_ids, log_prior, projs, blocks, turned):
    orients = class_ids.shape[0]
    return pl.pallas_call(
        functools.partial(score_kernel, blocks, turned),
        out_shape=jax.ShapeDtypeStruct((orients, data.shape[0]), jnp.float32),
        compiler_params=pltpu.CompilerParams(vmem_limit_bytes=8 * 2**20),
        name="score",
    )(data, allowed, class_ids.reshape(1, -1), log_prior.reshape(1, -1), *projs)


def back_kernel(parts, data_ref, *refs):
    part_refs, (best_ref, own_ref, *away_refs) = refs[:parts], refs[parts:]
    share = best_ref.shape[1]
    sums = [ref[...] for ref in part_refs]
    if parts == 4:
        part = dict(zip((0,) + SHARE, sums))
        rows = (part[0] + part[1]) + (part[2] + part[3])
    else:
        rows = sums[0]
    expo = jnp.exp(rows - jnp.max(rows, axis=0, keepdims=True))
    inverse = 1.0 / jnp.sum(expo, axis=0, keepdims=True)
    weights = (expo * inverse).astype(jnp.bfloat16)
    place = lax.axis_index(("shell", "sub"))
    best = inverse[:, 0:share]
    for piece in range(1, rows.shape[1] // share):
        best = jnp.where(place == piece, inverse[:, piece * share : (piece + 1) * share], best)
    best_ref[...] = best
    back = jnp.dot(weights, data_ref[...], preferred_element_type=jnp.float32)
    each = own_ref.shape[0]
    own_ref[...] = back[0:each]
    for k, ref in enumerate(away_refs):
        ref[...] = back[(k + 1) * each : (k + 2) * each].astype(ref.dtype)


def back(data, parts, away, pieces):
    orients, count = parts[0].shape
    each = orients // (away + 1)
    wide = data.shape[1]
    return pl.pallas_call(
        functools.partial(back_kernel, len(parts)),
        out_shape=[
            pltpu.VMEM((1, count // pieces), jnp.float32),
            jax.ShapeDtypeStruct((each, wide), jnp.float32),
        ]
        + [jax.ShapeDtypeStruct((each, wide), jnp.bfloat16)] * away,
        in_specs=[pl.BlockSpec(memory_space=pltpu.VMEM)] * (1 + len(parts)),
        out_specs=[pl.BlockSpec(memory_space=pltpu.VMEM)] * (2 + away),
        compiler_params=pltpu.CompilerParams(vmem_limit_bytes=8 * 2**20),
        name="back",
    )(data, *parts)


def finish_kernel(found_ref, own_ref, *refs):
    *away_refs, data_ref, weight_ref, best_ref = refs
    best_ref[...] = found_ref[0, :]
    pix = weight_ref.shape[1]
    total = own_ref[...]
    for ref in away_refs:
        total = total + ref[...].astype(jnp.float32)
    data_ref[:, 0, :] = total[:, :pix]
    data_ref[:, 1, :] = total[:, pix : 2 * pix]
    weight_ref[...] = total[:, 2 * pix :]


def finish(found, own, away):
    each, wide = own.shape
    return pl.pallas_call(
        finish_kernel,
        out_shape=[
            jax.ShapeDtypeStruct((each, 2, wide // 3), jnp.float32),
            jax.ShapeDtypeStruct((each, wide // 3), jnp.float32),
            jax.ShapeDtypeStruct(found.shape[1:], jnp.float32),
        ],
        compiler_params=pltpu.CompilerParams(vmem_limit_bytes=8 * 2**20),
        name="finish",
    )(found, own, *away)


def opening_kernel(out_ref):
    out_ref[...] = jnp.zeros_like(out_ref)


def opening():
    return pl.pallas_call(
        opening_kernel,
        out_specs=pl.BlockSpec(memory_space=pltpu.VMEM),
        out_shape=pltpu.VMEM((8, 128), jnp.float32),
        compiler_params=pltpu.CompilerParams(vmem_limit_bytes=2**20, has_side_effects=True),
        cost_estimate=pl.CostEstimate(flops=10**10, bytes_accessed=10**7, transcendentals=0),
        name="opening",
    )()


def rotate(value, axis, size, by):
    return lax.ppermute(value, axis, [((j + by) % size, j) for j in range(size)])


def swap(value, axes, size, mask):
    return lax.ppermute(value, axes, [(j ^ mask, j) for j in range(size)])


def body(images, ctf, projections, shifts, inv_sigma2, class_ids, log_prior, allowed):
    blocks = lax.axis_size("blk")
    pieces = lax.axis_size(("shell", "sub"))
    direct = blocks in FETCH

    first = opening()
    projections, first = lax.optimization_barrier((projections, first))
    if direct:
        projs = [projections] + [swap(projections, "blk", blocks, k) for k in FETCH[blocks]]
    else:
        projs = [lax.all_gather(projections, "blk", axis=0, tiled=True)]
    data = prepare(images, ctf, shifts, inv_sigma2, pieces, first)
    part = score(data, allowed, class_ids, log_prior, projs, blocks, direct)
    if pieces == 4:
        parts = [part] + [swap(part, ("shell", "sub"), 4, mask) for mask in SHARE]
    else:
        parts = [lax.psum(part, ("shell", "sub"))]
    best, own, *away = back(data, parts, blocks - 1 if direct else 0, pieces)
    if not direct:
        own = lax.psum_scatter(own, "blk", scatter_dimension=0, tiled=True)
    arrived = [rotate(away[k - 1], "blk", blocks, blocks - k) for k in (RETURN[blocks] if direct else ())]
    return finish(best, own, arrived)


def solution(mesh):
    in_specs = (
        P(("groups", "blk"), None, ("shell", "sub")),
        P(("groups", "blk"), ("shell", "sub")),
        P(("groups", "blk"), None, ("shell", "sub")),
        P(("groups", "blk"), None),
        P(("shell", "sub")),
        P("groups"),
        P(),
        P(("groups", "blk"), None),
    )
    out_specs = (
        P(("groups", "blk"), None, ("shell", "sub")),
        P(("groups", "blk"), ("shell", "sub")),
        P(("groups", "blk", "shell", "sub")),
    )
    return jax.shard_map(body, mesh=mesh, in_specs=in_specs, out_specs=out_specs, check_vma=False)
```

```python
import functools
import math

import jax
import jax.numpy as jnp
import ml_dtypes
import numpy as np
from jax import lax
from jax.experimental import pallas as pl
from jax.experimental.pallas import tpu as pltpu
from jax.sharding import PartitionSpec as P

KMAX = 64
BOX = 360
CLASSES = 4
PIXC = 8192
ROW = 2 * KMAX
REACH = 8
GROUP = 16
FETCH = {2: (1,), 4: (1, 3, 2)}
RETURN = {2: (1,), 4: (1, 2, 3)}
SHARE = (1, 2, 3)
SPLITS = 3


def split_terms(table):
    terms = []
    rest = table.astype(np.float64)
    for _ in range(SPLITS):
        term = rest.astype(ml_dtypes.bfloat16)
        terms.append(term)
        rest = rest - term.astype(np.float64)
    return np.concatenate(terms, axis=0)


@functools.lru_cache(maxsize=None)
def phase_table(pieces, rows):
    shift = np.arange(-REACH, REACH, dtype=np.float64)[:, None]
    unit = 2.0 * math.pi / BOX
    along_y = unit * shift * np.arange(-KMAX, KMAX, dtype=np.float64)[None, :]
    step = np.broadcast_to(unit * shift, along_y.shape)
    half = SPLITS * 2 * REACH
    tables = []
    for piece in range(pieces):
        first = step * (piece * rows)
        left = split_terms(np.concatenate([np.cos(first), np.sin(first), np.cos(step), np.sin(step)], axis=1))
        right = split_terms(np.concatenate([np.cos(along_y), np.sin(along_y)], axis=1))
        table = np.zeros((128, 6 * ROW), ml_dtypes.bfloat16)
        table[:half, : 4 * ROW] = left
        table[64 : 64 + half, 4 * ROW :] = right
        tables.append(table)
    return np.stack(tables)


def prepare_kernel(
    rows, image_ref, ctf_ref, shift_ref, inv_ref, table_ref, first_ref, out_ref, phase_ref, even_ref, odd_ref
):
    images = ctf_ref.shape[0]
    lines = 2 * rows

    line = lax.broadcasted_iota(jnp.int32, (128, images), 0)
    inner = line & 63
    moves = jnp.where(line < 64, shift_ref[0:1, :], shift_ref[1:2, :]) + REACH
    hit = ((inner & (2 * REACH - 1)) == moves) & (inner < SPLITS * 2 * REACH)
    phase_ref[...] = lax.dot_general(
        jnp.where(hit, 1.0, 0.0).astype(jnp.bfloat16),
        table_ref[lax.axis_index(("shell", "sub"))],
        (((0,), (0,)), ((), ())),
        preferred_element_type=jnp.float32,
    )

    def spread(g, ref):
        for i in range(GROUP):
            line = pl.multiple_of((g * GROUP + i) * lines, lines)
            wide = image_ref[pl.ds(line, lines), :].astype(jnp.float32)
            for slab in range(lines // 8):
                ref[pl.ds((slab * GROUP + i) * 8, 8), :] = wide[8 * slab : 8 * slab + 8]

    def weigh(g, ref):
        start = pl.multiple_of(g * GROUP, GROUP)
        phase = phase_ref[pl.ds(start, GROUP), :]
        cos_a, sin_a, cos_s, sin_s, cos_b, sin_b = (phase[:, k * ROW : (k + 1) * ROW] for k in range(6))
        cos_0 = cos_a * cos_b - sin_a * sin_b
        sin_0 = sin_a * cos_b + cos_a * sin_b
        cos_1 = cos_0 * cos_s - sin_0 * sin_s
        sin_1 = sin_0 * cos_s + cos_0 * sin_s
        twice = 2.0 * cos_s
        for t in range(rows):
            lanes = slice(t * ROW, (t + 1) * ROW)
            line = 8 * GROUP * (t // 4) + 2 * (t % 4)
            real = ref[pl.ds(line, GROUP, stride=8), :]
            imag = ref[pl.ds(line + 1, GROUP, stride=8), :]
            ctf = ctf_ref[pl.ds(start, GROUP), lanes].astype(jnp.float32)
            factor = ctf * inv_ref[0:1, lanes]
            out_ref[g, t] = (factor * (real * cos_0 + imag * sin_0)).astype(jnp.bfloat16)
            out_ref[g, rows + t] = (factor * (imag * cos_0 - real * sin_0)).astype(jnp.bfloat16)
            out_ref[g, 2 * rows + t] = (factor * ctf).astype(jnp.bfloat16)
            cos_0, cos_1 = cos_1, twice * cos_1 - cos_0
            sin_0, sin_1 = sin_1, twice * sin_1 - sin_0

    def step(i, carry):
        spread(2 * i, even_ref)
        weigh(2 * i, even_ref)
        spread(2 * i + 1, odd_ref)
        weigh(2 * i + 1, odd_ref)
        return carry

    lax.fori_loop(0, images // (2 * GROUP), step, 0)


def prepare(images, ctf, shifts, inv_sigma2, pieces, first):
    count, _, pix = images.shape
    rows = pix // ROW
    flat = images.reshape(count, 2, rows, ROW).transpose(0, 2, 1, 3).reshape(count * rows * 2, ROW)
    args = (flat, ctf, shifts.T, inv_sigma2.reshape(1, pix), phase_table(pieces, rows), first)
    return pl.pallas_call(
        functools.partial(prepare_kernel, rows),
        in_specs=[pl.BlockSpec(memory_space=pltpu.VMEM)] * len(args),
        out_specs=pl.BlockSpec(memory_space=pltpu.VMEM),
        out_shape=pltpu.VMEM((count // GROUP, 3 * rows, GROUP, ROW), jnp.bfloat16),
        scratch_shapes=[
            pltpu.VMEM((count, 6 * ROW), jnp.float32),
            pltpu.VMEM((2 * rows * GROUP, ROW), jnp.float32),
            pltpu.VMEM((2 * rows * GROUP, ROW), jnp.float32),
        ],
        compiler_params=pltpu.CompilerParams(vmem_limit_bytes=8 * 2**20),
        name="prepare",
    )(*[pltpu.with_memory_space_constraint(jnp.asarray(arg), pltpu.VMEM) for arg in args])


def whole(data_ref):
    groups, columns, _, _ = data_ref.shape
    return jnp.concatenate([data_ref[:, k].reshape(groups * GROUP, ROW) for k in range(columns)], axis=1)


def score_kernel(blocks, turned, data_ref, allowed_ref, class_ref, prior_ref, *refs):
    *proj_refs, out_ref = refs
    orients = out_ref.shape[0]
    each = orients // blocks
    me = lax.axis_index("blk") if turned else 0

    line = lax.broadcasted_iota(jnp.int32, (orients, orients), 0)
    lane = lax.broadcasted_iota(jnp.int32, (orients, orients), 1)
    block = lax.rem(line // each + me, blocks)
    own = lane == block * each + lax.rem(line, each)
    prior = jnp.zeros((orients, orients), jnp.float32)
    for c in range(CLASSES):
        prior = jnp.where(own & (class_ref[...] == c), prior_ref[0:1, c : c + 1], prior)
    bias = jnp.sum(prior, axis=1, keepdims=True)
    listed = jnp.zeros((orients, 1), jnp.bool_)
    for k in range(allowed_ref.shape[1]):
        listed = listed | (block[:, 0:1] == allowed_ref[0:1, k : k + 1])
    bias = jnp.where(listed, bias, jnp.float32(-1e30))
    bias = jnp.where(lax.axis_index(("shell", "sub")) == 0, bias, 0.0)

    parts = []
    for ref in proj_refs:
        wide = ref[...].astype(jnp.float32)
        real, imag = wide[:, 0, :], wide[:, 1, :]
        parts.append(jnp.concatenate([2.0 * real, 2.0 * imag, -(real * real + imag * imag)], axis=1))
    joint = jnp.concatenate(parts, axis=0).astype(jnp.bfloat16)
    raw = lax.dot_general(joint, whole(data_ref), (((1,), (1,)), ((), ())), preferred_element_type=jnp.float32)
    if turned:
        came = [raw[:each]] * blocks
        for k, mask in enumerate(FETCH[blocks], start=1):
            came[mask] = raw[k * each : (k + 1) * each]
        leave = came[:1]
        for k in range(1, blocks):
            at = lax.rem(me + k, blocks) ^ me
            value = came[1]
            for other in range(2, blocks):
                value = jnp.where(at == other, came[other], value)
            leave.append(value)
        raw = jnp.concatenate(leave, axis=0)
    out_ref[...] = raw * (1.0 / math.sqrt(PIXC)) + bias


def score(data, allowed, class_ids, log_prior, projs, blocks, turned):
    orients = class_ids.shape[0]
    return pl.pallas_call(
        functools.partial(score_kernel, blocks, turned),
        out_shape=jax.ShapeDtypeStruct((orients, data.shape[0] * GROUP), jnp.float32),
        compiler_params=pltpu.CompilerParams(vmem_limit_bytes=8 * 2**20),
        name="score",
    )(data, allowed, class_ids.reshape(1, -1), log_prior.reshape(1, -1), *projs)


def back_kernel(parts, data_ref, *refs):
    part_refs, (best_ref, own_ref, *away_refs) = refs[:parts], refs[parts:]
    share = best_ref.shape[1]
    sums = [ref[...] for ref in part_refs]
    if parts == 4:
        part = dict(zip((0,) + SHARE, sums))
        rows = (part[0] + part[1]) + (part[2] + part[3])
    else:
        rows = sums[0]
    expo = jnp.exp(rows - jnp.max(rows, axis=0, keepdims=True))
    inverse = 1.0 / jnp.sum(expo, axis=0, keepdims=True)
    weights = (expo * inverse).astype(jnp.bfloat16)
    place = lax.axis_index(("shell", "sub"))
    best = inverse[:, 0:share]
    for piece in range(1, rows.shape[1] // share):
        best = jnp.where(place == piece, inverse[:, piece * share : (piece + 1) * share], best)
    best_ref[...] = best
    back = jnp.dot(weights, whole(data_ref), preferred_element_type=jnp.float32)
    each = own_ref.shape[0]
    own_ref[...] = back[0:each]
    for k, ref in enumerate(away_refs):
        ref[...] = back[(k + 1) * each : (k + 2) * each].astype(ref.dtype)


def back(data, parts, away, pieces):
    orients, count = parts[0].shape
    each = orients // (away + 1)
    wide = data.shape[1] * ROW
    return pl.pallas_call(
        functools.partial(back_kernel, len(parts)),
        out_shape=[
            pltpu.VMEM((1, count // pieces), jnp.float32),
            jax.ShapeDtypeStruct((each, wide), jnp.float32),
        ]
        + [jax.ShapeDtypeStruct((each, wide), jnp.bfloat16)] * away,
        in_specs=[pl.BlockSpec(memory_space=pltpu.VMEM)] * (1 + len(parts)),
        out_specs=[pl.BlockSpec(memory_space=pltpu.VMEM)] * (2 + away),
        compiler_params=pltpu.CompilerParams(vmem_limit_bytes=8 * 2**20),
        name="back",
    )(data, *parts)


def finish_kernel(found_ref, own_ref, *refs):
    *away_refs, data_ref, weight_ref, best_ref = refs
    best_ref[...] = found_ref[0, :]
    pix = weight_ref.shape[1]
    total = own_ref[...]
    for ref in away_refs:
        total = total + ref[...].astype(jnp.float32)
    data_ref[:, 0, :] = total[:, :pix]
    data_ref[:, 1, :] = total[:, pix : 2 * pix]
    weight_ref[...] = total[:, 2 * pix :]


def finish(found, own, away):
    each, wide = own.shape
    return pl.pallas_call(
        finish_kernel,
        out_shape=[
            jax.ShapeDtypeStruct((each, 2, wide // 3), jnp.float32),
            jax.ShapeDtypeStruct((each, wide // 3), jnp.float32),
            jax.ShapeDtypeStruct(found.shape[1:], jnp.float32),
        ],
        compiler_params=pltpu.CompilerParams(vmem_limit_bytes=8 * 2**20),
        name="finish",
    )(found, own, *away)


def opening_kernel(out_ref):
    out_ref[...] = jnp.zeros_like(out_ref)


def opening():
    return pl.pallas_call(
        opening_kernel,
        out_specs=pl.BlockSpec(memory_space=pltpu.VMEM),
        out_shape=pltpu.VMEM((8, 128), jnp.float32),
        compiler_params=pltpu.CompilerParams(vmem_limit_bytes=2**20, has_side_effects=True),
        cost_estimate=pl.CostEstimate(flops=10**10, bytes_accessed=10**7, transcendentals=0),
        name="opening",
    )()


def rotate(value, axis, size, by):
    return lax.ppermute(value, axis, [((j + by) % size, j) for j in range(size)])


def swap(value, axes, size, mask):
    return lax.ppermute(value, axes, [(j ^ mask, j) for j in range(size)])


def body(images, ctf, projections, shifts, inv_sigma2, class_ids, log_prior, allowed):
    blocks = lax.axis_size("blk")
    pieces = lax.axis_size(("shell", "sub"))
    direct = blocks in FETCH

    first = opening()
    projections, first = lax.optimization_barrier((projections, first))
    if direct:
        projs = [projections] + [swap(projections, "blk", blocks, k) for k in FETCH[blocks]]
    else:
        projs = [lax.all_gather(projections, "blk", axis=0, tiled=True)]
    data = prepare(images, ctf, shifts, inv_sigma2, pieces, first)
    part = score(data, allowed, class_ids, log_prior, projs, blocks, direct)
    if pieces == 4:
        parts = [part] + [swap(part, ("shell", "sub"), 4, mask) for mask in SHARE]
    else:
        parts = [lax.psum(part, ("shell", "sub"))]
    best, own, *away = back(data, parts, blocks - 1 if direct else 0, pieces)
    if not direct:
        own = lax.psum_scatter(own, "blk", scatter_dimension=0, tiled=True)
    arrived = [rotate(away[k - 1], "blk", blocks, blocks - k) for k in (RETURN[blocks] if direct else ())]
    return finish(best, own, arrived)


def solution(mesh):
    in_specs = (
        P(("groups", "blk"), None, ("shell", "sub")),
        P(("groups", "blk"), ("shell", "sub")),
        P(("groups", "blk"), None, ("shell", "sub")),
        P(("groups", "blk"), None),
        P(("shell", "sub")),
        P("groups"),
        P(),
        P(("groups", "blk"), None),
    )
    out_specs = (
        P(("groups", "blk"), None, ("shell", "sub")),
        P(("groups", "blk"), ("shell", "sub")),
        P(("groups", "blk", "shell", "sub")),
    )
    return jax.shard_map(body, mesh=mesh, in_specs=in_specs, out_specs=out_specs, check_vma=False)
```

```python
import functools
import math

import jax
import jax.numpy as jnp
import ml_dtypes
import numpy as np
from jax import lax
from jax.experimental import pallas as pl
from jax.experimental.pallas import tpu as pltpu
from jax.sharding import PartitionSpec as P

KMAX = 64
BOX = 360
CLASSES = 4
PIXC = 8192
ROW = 2 * KMAX
REACH = 8
GROUP = 16
FETCH = {2: ((1, 0),), 4: ((1, 0, 3, 2), (2, 3, 1, 0), (3, 2, 0, 1))}
RETURN = {2: ((1, 0),), 4: ((1, 2, 3, 0), (2, 3, 0, 1), (3, 0, 1, 2))}
SHARE = (1, 2, 3)
SPLITS = 3


def split_terms(table):
    terms = []
    rest = table.astype(np.float64)
    for _ in range(SPLITS):
        term = rest.astype(ml_dtypes.bfloat16)
        terms.append(term)
        rest = rest - term.astype(np.float64)
    return np.concatenate(terms, axis=0)


@functools.lru_cache(maxsize=None)
def phase_table(pieces, rows):
    shift = np.arange(-REACH, REACH, dtype=np.float64)[:, None]
    unit = 2.0 * math.pi / BOX
    along_y = unit * shift * np.arange(-KMAX, KMAX, dtype=np.float64)[None, :]
    step = np.broadcast_to(unit * shift, along_y.shape)
    half = SPLITS * 2 * REACH
    tables = []
    for piece in range(pieces):
        first = step * (piece * rows)
        left = split_terms(np.concatenate([np.cos(first), np.sin(first), np.cos(step), np.sin(step)], axis=1))
        right = split_terms(np.concatenate([np.cos(along_y), np.sin(along_y)], axis=1))
        table = np.zeros((128, 6 * ROW), ml_dtypes.bfloat16)
        table[:half, : 4 * ROW] = left
        table[64 : 64 + half, 4 * ROW :] = right
        tables.append(table)
    return np.stack(tables)


def prepare_kernel(
    rows, image_ref, ctf_ref, shift_ref, inv_ref, table_ref, first_ref, out_ref, phase_ref, even_ref, odd_ref
):
    images = ctf_ref.shape[0]
    lines = 2 * rows

    line = lax.broadcasted_iota(jnp.int32, (128, images), 0)
    inner = line & 63
    moves = jnp.where(line < 64, shift_ref[0:1, :], shift_ref[1:2, :]) + REACH
    hit = ((inner & (2 * REACH - 1)) == moves) & (inner < SPLITS * 2 * REACH)
    phase_ref[...] = lax.dot_general(
        jnp.where(hit, 1.0, 0.0).astype(jnp.bfloat16),
        table_ref[lax.axis_index(("shell", "sub"))],
        (((0,), (0,)), ((), ())),
        preferred_element_type=jnp.float32,
    )

    def spread(g, ref):
        for i in range(GROUP):
            line = pl.multiple_of((g * GROUP + i) * lines, lines)
            wide = image_ref[pl.ds(line, lines), :].astype(jnp.float32)
            for slab in range(lines // 8):
                ref[pl.ds((slab * GROUP + i) * 8, 8), :] = wide[8 * slab : 8 * slab + 8]

    def weigh(g, ref):
        start = pl.multiple_of(g * GROUP, GROUP)
        phase = phase_ref[pl.ds(start, GROUP), :]
        cos_a, sin_a, cos_s, sin_s, cos_b, sin_b = (phase[:, k * ROW : (k + 1) * ROW] for k in range(6))
        cos_0 = cos_a * cos_b - sin_a * sin_b
        sin_0 = sin_a * cos_b + cos_a * sin_b
        cos_1 = cos_0 * cos_s - sin_0 * sin_s
        sin_1 = sin_0 * cos_s + cos_0 * sin_s
        twice = 2.0 * cos_s
        for t in range(rows):
            lanes = slice(t * ROW, (t + 1) * ROW)
            line = 8 * GROUP * (t // 4) + 2 * (t % 4)
            real = ref[pl.ds(line, GROUP, stride=8), :]
            imag = ref[pl.ds(line + 1, GROUP, stride=8), :]
            ctf = ctf_ref[pl.ds(start, GROUP), lanes].astype(jnp.float32)
            factor = ctf * inv_ref[0:1, lanes]
            out_ref[g, t] = (factor * (real * cos_0 + imag * sin_0)).astype(jnp.bfloat16)
            out_ref[g, rows + t] = (factor * (imag * cos_0 - real * sin_0)).astype(jnp.bfloat16)
            out_ref[g, 2 * rows + t] = (factor * ctf).astype(jnp.bfloat16)
            cos_0, cos_1 = cos_1, twice * cos_1 - cos_0
            sin_0, sin_1 = sin_1, twice * sin_1 - sin_0

    def step(i, carry):
        spread(2 * i, even_ref)
        weigh(2 * i, even_ref)
        spread(2 * i + 1, odd_ref)
        weigh(2 * i + 1, odd_ref)
        return carry

    lax.fori_loop(0, images // (2 * GROUP), step, 0)


def prepare(images, ctf, shifts, inv_sigma2, pieces, first):
    count, _, pix = images.shape
    rows = pix // ROW
    flat = images.reshape(count, 2, rows, ROW).transpose(0, 2, 1, 3).reshape(count * rows * 2, ROW)
    args = (flat, ctf, shifts.T, inv_sigma2.reshape(1, pix), phase_table(pieces, rows), first)
    return pl.pallas_call(
        functools.partial(prepare_kernel, rows),
        in_specs=[pl.BlockSpec(memory_space=pltpu.VMEM)] * len(args),
        out_specs=pl.BlockSpec(memory_space=pltpu.VMEM),
        out_shape=pltpu.VMEM((count // GROUP, 3 * rows, GROUP, ROW), jnp.bfloat16),
        scratch_shapes=[
            pltpu.VMEM((count, 6 * ROW), jnp.float32),
            pltpu.VMEM((2 * rows * GROUP, ROW), jnp.float32),
            pltpu.VMEM((2 * rows * GROUP, ROW), jnp.float32),
        ],
        compiler_params=pltpu.CompilerParams(vmem_limit_bytes=8 * 2**20),
        name="prepare",
    )(*[pltpu.with_memory_space_constraint(jnp.asarray(arg), pltpu.VMEM) for arg in args])


def whole(data_ref):
    groups, columns, _, _ = data_ref.shape
    return jnp.concatenate([data_ref[:, k].reshape(groups * GROUP, ROW) for k in range(columns)], axis=1)


def score_kernel(blocks, turned, data_ref, allowed_ref, class_ref, prior_ref, *refs):
    *proj_refs, out_ref = refs
    orients = out_ref.shape[0]
    each = orients // blocks
    me = lax.axis_index("blk") if turned else 0

    line = lax.broadcasted_iota(jnp.int32, (orients, orients), 0)
    lane = lax.broadcasted_iota(jnp.int32, (orients, orients), 1)
    block = line // each
    if turned:
        slot = block
        block = jnp.where(slot == 0, me, 0)
        for k in range(1, blocks):
            block = jnp.where(slot == k, entry(RETURN[blocks][k - 1], me), block)
    own = lane == block * each + lax.rem(line, each)
    prior = jnp.zeros((orients, orients), jnp.float32)
    for c in range(CLASSES):
        prior = jnp.where(own & (class_ref[...] == c), prior_ref[0:1, c : c + 1], prior)
    bias = jnp.sum(prior, axis=1, keepdims=True)
    listed = jnp.zeros((orients, 1), jnp.bool_)
    for k in range(allowed_ref.shape[1]):
        listed = listed | (block[:, 0:1] == allowed_ref[0:1, k : k + 1])
    bias = jnp.where(listed, bias, jnp.float32(-1e30))
    bias = jnp.where(lax.axis_index(("shell", "sub")) == 0, bias, 0.0)

    parts = []
    for ref in proj_refs:
        wide = ref[...].astype(jnp.float32)
        real, imag = wide[:, 0, :], wide[:, 1, :]
        parts.append(jnp.concatenate([2.0 * real, 2.0 * imag, -(real * real + imag * imag)], axis=1))
    joint = jnp.concatenate(parts, axis=0).astype(jnp.bfloat16)
    raw = lax.dot_general(joint, whole(data_ref), (((1,), (1,)), ((), ())), preferred_element_type=jnp.float32)
    if turned:
        came = [raw[k * each : (k + 1) * each] for k in range(blocks)]
        leave = came[:1]
        for k in range(1, blocks):
            value = came[1]
            for other in range(2, blocks):
                value = jnp.where(entry(FETCH[blocks][other - 1], me) == entry(RETURN[blocks][k - 1], me), came[other], value)
            leave.append(value)
        raw = jnp.concatenate(leave, axis=0)
    out_ref[...] = raw * (1.0 / math.sqrt(PIXC)) + bias


def score(data, allowed, class_ids, log_prior, projs, blocks, turned):
    orients = class_ids.shape[0]
    return pl.pallas_call(
        functools.partial(score_kernel, blocks, turned),
        out_shape=jax.ShapeDtypeStruct((orients, data.shape[0] * GROUP), jnp.float32),
        compiler_params=pltpu.CompilerParams(vmem_limit_bytes=8 * 2**20),
        name="score",
    )(data, allowed, class_ids.reshape(1, -1), log_prior.reshape(1, -1), *projs)


def back_kernel(parts, data_ref, *refs):
    part_refs, (best_ref, own_ref, *away_refs) = refs[:parts], refs[parts:]
    share = best_ref.shape[1]
    sums = [ref[...] for ref in part_refs]
    if parts == 4:
        part = dict(zip((0,) + SHARE, sums))
        rows = (part[0] + part[1]) + (part[2] + part[3])
    else:
        rows = sums[0]
    expo = jnp.exp(rows - jnp.max(rows, axis=0, keepdims=True))
    inverse = 1.0 / jnp.sum(expo, axis=0, keepdims=True)
    weights = (expo * inverse).astype(jnp.bfloat16)
    place = lax.axis_index(("shell", "sub"))
    best = inverse[:, 0:share]
    for piece in range(1, rows.shape[1] // share):
        best = jnp.where(place == piece, inverse[:, piece * share : (piece + 1) * share], best)
    best_ref[...] = best
    back = jnp.dot(weights, whole(data_ref), preferred_element_type=jnp.float32)
    each = own_ref.shape[0]
    own_ref[...] = back[0:each]
    for k, ref in enumerate(away_refs):
        ref[...] = back[(k + 1) * each : (k + 2) * each].astype(ref.dtype)


def back(data, parts, away, pieces):
    orients, count = parts[0].shape
    each = orients // (away + 1)
    wide = data.shape[1] * ROW
    return pl.pallas_call(
        functools.partial(back_kernel, len(parts)),
        out_shape=[
            pltpu.VMEM((1, count // pieces), jnp.float32),
            jax.ShapeDtypeStruct((each, wide), jnp.float32),
        ]
        + [jax.ShapeDtypeStruct((each, wide), jnp.bfloat16)] * away,
        in_specs=[pl.BlockSpec(memory_space=pltpu.VMEM)] * (1 + len(parts)),
        out_specs=[pl.BlockSpec(memory_space=pltpu.VMEM)] * (2 + away),
        compiler_params=pltpu.CompilerParams(vmem_limit_bytes=8 * 2**20),
        name="back",
    )(data, *parts)


def finish_kernel(found_ref, own_ref, *refs):
    *away_refs, data_ref, weight_ref, best_ref = refs
    best_ref[...] = found_ref[0, :]
    pix = weight_ref.shape[1]
    total = own_ref[...]
    for ref in away_refs:
        total = total + ref[...].astype(jnp.float32)
    data_ref[:, 0, :] = total[:, :pix]
    data_ref[:, 1, :] = total[:, pix : 2 * pix]
    weight_ref[...] = total[:, 2 * pix :]


def finish(found, own, away):
    each, wide = own.shape
    return pl.pallas_call(
        finish_kernel,
        out_shape=[
            jax.ShapeDtypeStruct((each, 2, wide // 3), jnp.float32),
            jax.ShapeDtypeStruct((each, wide // 3), jnp.float32),
            jax.ShapeDtypeStruct(found.shape[1:], jnp.float32),
        ],
        compiler_params=pltpu.CompilerParams(vmem_limit_bytes=8 * 2**20),
        name="finish",
    )(found, own, *away)


def opening_kernel(out_ref):
    out_ref[...] = jnp.zeros_like(out_ref)


def opening():
    return pl.pallas_call(
        opening_kernel,
        out_specs=pl.BlockSpec(memory_space=pltpu.VMEM),
        out_shape=pltpu.VMEM((8, 128), jnp.float32),
        compiler_params=pltpu.CompilerParams(vmem_limit_bytes=2**20, has_side_effects=True),
        cost_estimate=pl.CostEstimate(flops=10**10, bytes_accessed=10**7, transcendentals=0),
        name="opening",
    )()


def entry(table, me):
    value = jnp.int32(table[0])
    for j in range(1, len(table)):
        value = jnp.where(me == j, jnp.int32(table[j]), value)
    return value


def swap(value, axes, size, mask):
    return lax.ppermute(value, axes, [(j ^ mask, j) for j in range(size)])


def body(images, ctf, projections, shifts, inv_sigma2, class_ids, log_prior, allowed):
    blocks = lax.axis_size("blk")
    pieces = lax.axis_size(("shell", "sub"))
    direct = blocks in FETCH

    first = opening()
    projections, first = lax.optimization_barrier((projections, first))
    if direct:
        projs = [projections] + [lax.ppermute(projections, "blk", [(source, j) for j, source in enumerate(sources)]) for sources in FETCH[blocks]]
    else:
        projs = [lax.all_gather(projections, "blk", axis=0, tiled=True)]
    data = prepare(images, ctf, shifts, inv_sigma2, pieces, first)
    part = score(data, allowed, class_ids, log_prior, projs, blocks, direct)
    if pieces == 4:
        parts = [part] + [swap(part, ("shell", "sub"), 4, mask) for mask in SHARE]
    else:
        parts = [lax.psum(part, ("shell", "sub"))]
    best, own, *away = back(data, parts, blocks - 1 if direct else 0, pieces)
    if not direct:
        own = lax.psum_scatter(own, "blk", scatter_dimension=0, tiled=True)
    arrived = [
        lax.ppermute(value, "blk", list(enumerate(goals))) for value, goals in zip(away, RETURN[blocks] if direct else ())
    ]
    return finish(best, own, arrived)


def solution(mesh):
    in_specs = (
        P(("groups", "blk"), None, ("shell", "sub")),
        P(("groups", "blk"), ("shell", "sub")),
        P(("groups", "blk"), None, ("shell", "sub")),
        P(("groups", "blk"), None),
        P(("shell", "sub")),
        P("groups"),
        P(),
        P(("groups", "blk"), None),
    )
    out_specs = (
        P(("groups", "blk"), None, ("shell", "sub")),
        P(("groups", "blk"), ("shell", "sub")),
        P(("groups", "blk", "shell", "sub")),
    )
    return jax.shard_map(body, mesh=mesh, in_specs=in_specs, out_specs=out_specs, check_vma=False)
```

```python
import functools
import math

import jax
import jax.numpy as jnp
import ml_dtypes
import numpy as np
from jax import lax
from jax.experimental import pallas as pl
from jax.experimental.pallas import tpu as pltpu
from jax.sharding import PartitionSpec as P

KMAX = 64
BOX = 360
CLASSES = 4
PIXC = 8192
ROW = 2 * KMAX
REACH = 8
GROUP = 16
FETCH = {2: ((1, 0),), 4: ((1, 0, 3, 2), (2, 3, 1, 0), (3, 2, 0, 1))}
RETURN = {2: ((1, 0),), 4: ((1, 2, 3, 0), (2, 3, 0, 1), (3, 0, 1, 2))}
SHARE = (1, 2, 3)
SPLITS = 3


def split_terms(table):
    terms = []
    rest = table.astype(np.float64)
    for _ in range(SPLITS):
        term = rest.astype(ml_dtypes.bfloat16)
        terms.append(term)
        rest = rest - term.astype(np.float64)
    return np.concatenate(terms, axis=0)


@functools.lru_cache(maxsize=None)
def phase_table(pieces, rows):
    shift = np.arange(-REACH, REACH, dtype=np.float64)[:, None]
    unit = 2.0 * math.pi / BOX
    along_y = unit * shift * np.arange(-KMAX, KMAX, dtype=np.float64)[None, :]
    step = np.broadcast_to(unit * shift, along_y.shape)
    half = SPLITS * 2 * REACH
    tables = []
    for piece in range(pieces):
        first = step * (piece * rows)
        left = split_terms(np.concatenate([np.cos(first), np.sin(first), np.cos(step), np.sin(step)], axis=1))
        right = split_terms(np.concatenate([np.cos(along_y), np.sin(along_y)], axis=1))
        table = np.zeros((128, 6 * ROW), ml_dtypes.bfloat16)
        table[:half, : 4 * ROW] = left
        table[64 : 64 + half, 4 * ROW :] = right
        tables.append(table)
    return np.stack(tables)


def prepare_kernel(
    rows, image_ref, ctf_ref, shift_ref, inv_ref, table_ref, first_ref, out_ref, phase_ref, even_ref, odd_ref
):
    images = ctf_ref.shape[0]
    lines = 2 * rows

    line = lax.broadcasted_iota(jnp.int32, (128, images), 0)
    inner = line & 63
    moves = jnp.where(line < 64, shift_ref[0:1, :], shift_ref[1:2, :]) + REACH
    hit = ((inner & (2 * REACH - 1)) == moves) & (inner < SPLITS * 2 * REACH)
    phase_ref[...] = lax.dot_general(
        jnp.where(hit, 1.0, 0.0).astype(jnp.bfloat16),
        table_ref[lax.axis_index(("shell", "sub"))],
        (((0,), (0,)), ((), ())),
        preferred_element_type=jnp.float32,
    )

    def spread(g, ref):
        for i in range(GROUP):
            line = pl.multiple_of((g * GROUP + i) * lines, lines)
            wide = image_ref[pl.ds(line, lines), :].astype(jnp.float32)
            for slab in range(lines // 8):
                ref[pl.ds((slab * GROUP + i) * 8, 8), :] = wide[8 * slab : 8 * slab + 8]

    def weigh(g, ref):
        start = pl.multiple_of(g * GROUP, GROUP)
        phase = phase_ref[pl.ds(start, GROUP), :]
        cos_a, sin_a, cos_s, sin_s, cos_b, sin_b = (phase[:, k * ROW : (k + 1) * ROW] for k in range(6))
        cos_0 = cos_a * cos_b - sin_a * sin_b
        sin_0 = sin_a * cos_b + cos_a * sin_b
        cos_1 = cos_0 * cos_s - sin_0 * sin_s
        sin_1 = sin_0 * cos_s + cos_0 * sin_s
        twice = 2.0 * cos_s
        for t in range(rows):
            lanes = slice(t * ROW, (t + 1) * ROW)
            line = 8 * GROUP * (t // 4) + 2 * (t % 4)
            real = ref[pl.ds(line, GROUP, stride=8), :]
            imag = ref[pl.ds(line + 1, GROUP, stride=8), :]
            ctf = ctf_ref[pl.ds(start, GROUP), lanes].astype(jnp.float32)
            factor = ctf * inv_ref[0:1, lanes]
            out_ref[g, t] = (factor * (real * cos_0 + imag * sin_0)).astype(jnp.bfloat16)
            out_ref[g, rows + t] = (factor * (imag * cos_0 - real * sin_0)).astype(jnp.bfloat16)
            out_ref[g, 2 * rows + t] = (factor * ctf).astype(jnp.bfloat16)
            cos_0, cos_1 = cos_1, twice * cos_1 - cos_0
            sin_0, sin_1 = sin_1, twice * sin_1 - sin_0

    def step(i, carry):
        spread(2 * i, even_ref)
        weigh(2 * i, even_ref)
        spread(2 * i + 1, odd_ref)
        weigh(2 * i + 1, odd_ref)
        return carry

    lax.fori_loop(0, images // (2 * GROUP), step, 0)


def prepare(images, ctf, shifts, inv_sigma2, pieces, first):
    count, _, pix = images.shape
    rows = pix // ROW
    flat = images.reshape(count, 2, rows, ROW).transpose(0, 2, 1, 3).reshape(count * rows * 2, ROW)
    args = (flat, ctf, shifts.T, inv_sigma2.reshape(1, pix), phase_table(pieces, rows), first)
    return pl.pallas_call(
        functools.partial(prepare_kernel, rows),
        in_specs=[pl.BlockSpec(memory_space=pltpu.VMEM)] * len(args),
        out_specs=pl.BlockSpec(memory_space=pltpu.VMEM),
        out_shape=pltpu.VMEM((count // GROUP, 3 * rows, GROUP, ROW), jnp.bfloat16),
        scratch_shapes=[
            pltpu.VMEM((count, 6 * ROW), jnp.float32),
            pltpu.VMEM((2 * rows * GROUP, ROW), jnp.float32),
            pltpu.VMEM((2 * rows * GROUP, ROW), jnp.float32),
        ],
        compiler_params=pltpu.CompilerParams(vmem_limit_bytes=8 * 2**20),
        name="prepare",
    )(*[pltpu.with_memory_space_constraint(jnp.asarray(arg), pltpu.VMEM) for arg in args])


def whole(data_ref):
    groups, columns, _, _ = data_ref.shape
    return jnp.concatenate([data_ref[:, k].reshape(groups * GROUP, ROW) for k in range(columns)], axis=1)


def score_kernel(blocks, turned, data_ref, allowed_ref, class_ref, prior_ref, *refs):
    *proj_refs, out_ref = refs
    orients = out_ref.shape[0]
    each = orients // blocks
    me = lax.axis_index("blk") if turned else 0

    line = lax.broadcasted_iota(jnp.int32, (orients, orients), 0)
    lane = lax.broadcasted_iota(jnp.int32, (orients, orients), 1)
    block = line // each
    if turned:
        slot = block
        block = jnp.where(slot == 0, me, 0)
        for k in range(1, blocks):
            block = jnp.where(slot == k, entry(RETURN[blocks][k - 1], me), block)
    own = lane == block * each + lax.rem(line, each)
    prior = jnp.zeros((orients, orients), jnp.float32)
    for c in range(CLASSES):
        prior = jnp.where(own & (class_ref[...] == c), prior_ref[0:1, c : c + 1], prior)
    bias = jnp.sum(prior, axis=1, keepdims=True)
    listed = jnp.zeros((orients, 1), jnp.bool_)
    for k in range(allowed_ref.shape[1]):
        listed = listed | (block[:, 0:1] == allowed_ref[0:1, k : k + 1])
    bias = jnp.where(listed, bias, jnp.float32(-1e30))
    bias = jnp.where(lax.axis_index(("shell", "sub")) == 0, bias, 0.0)

    parts = []
    for ref in proj_refs:
        real, imag = (ref[:, part, :].astype(jnp.float32) for part in range(2))
        parts.append(jnp.concatenate([2.0 * real, 2.0 * imag, -(real * real + imag * imag)], axis=1))
    joint = jnp.concatenate(parts, axis=0).astype(jnp.bfloat16)
    raw = lax.dot_general(joint, whole(data_ref), (((1,), (1,)), ((), ())), preferred_element_type=jnp.float32)
    if turned:
        came = [raw[k * each : (k + 1) * each] for k in range(blocks)]
        leave = came[:1]
        for k in range(1, blocks):
            value = came[1]
            for other in range(2, blocks):
                value = jnp.where(entry(FETCH[blocks][other - 1], me) == entry(RETURN[blocks][k - 1], me), came[other], value)
            leave.append(value)
        raw = jnp.concatenate(leave, axis=0)
    out_ref[...] = raw * (1.0 / math.sqrt(PIXC)) + bias


def score(data, allowed, class_ids, log_prior, projs, blocks, turned):
    orients = class_ids.shape[0]
    return pl.pallas_call(
        functools.partial(score_kernel, blocks, turned),
        out_shape=jax.ShapeDtypeStruct((orients, data.shape[0] * GROUP), jnp.float32),
        compiler_params=pltpu.CompilerParams(vmem_limit_bytes=8 * 2**20),
        name="score",
    )(data, allowed, class_ids.reshape(1, -1), log_prior.reshape(1, -1), *projs)


def back_kernel(parts, data_ref, *refs):
    part_refs, (best_ref, own_ref, *away_refs) = refs[:parts], refs[parts:]
    share = best_ref.shape[1]
    sums = [ref[...] for ref in part_refs]
    if parts == 4:
        part = dict(zip((0,) + SHARE, sums))
        rows = (part[0] + part[1]) + (part[2] + part[3])
    else:
        rows = sums[0]
    expo = jnp.exp(rows - jnp.max(rows, axis=0, keepdims=True))
    inverse = 1.0 / jnp.sum(expo, axis=0, keepdims=True)
    weights = (expo * inverse).astype(jnp.bfloat16)
    place = lax.axis_index(("shell", "sub"))
    best = inverse[:, 0:share]
    for piece in range(1, rows.shape[1] // share):
        best = jnp.where(place == piece, inverse[:, piece * share : (piece + 1) * share], best)
    best_ref[...] = best
    back = jnp.dot(weights, whole(data_ref), preferred_element_type=jnp.float32)
    each = own_ref.shape[0]
    own_ref[...] = back[0:each]
    for k, ref in enumerate(away_refs):
        ref[...] = back[(k + 1) * each : (k + 2) * each].astype(ref.dtype)


def back(data, parts, away, pieces):
    orients, count = parts[0].shape
    each = orients // (away + 1)
    wide = data.shape[1] * ROW
    return pl.pallas_call(
        functools.partial(back_kernel, len(parts)),
        out_shape=[
            pltpu.VMEM((1, count // pieces), jnp.float32),
            jax.ShapeDtypeStruct((each, wide), jnp.float32),
        ]
        + [jax.ShapeDtypeStruct((each, wide), jnp.bfloat16)] * away,
        in_specs=[pl.BlockSpec(memory_space=pltpu.VMEM)] * (1 + len(parts)),
        out_specs=[pl.BlockSpec(memory_space=pltpu.VMEM)] * (2 + away),
        compiler_params=pltpu.CompilerParams(vmem_limit_bytes=8 * 2**20),
        name="back",
    )(data, *parts)


def finish_kernel(found_ref, own_ref, *refs):
    *away_refs, data_ref, weight_ref, best_ref = refs
    best_ref[...] = found_ref[0, :]
    pix = weight_ref.shape[1]
    total = own_ref[...]
    for ref in away_refs:
        total = total + ref[...].astype(jnp.float32)
    data_ref[:, 0, :] = total[:, :pix]
    data_ref[:, 1, :] = total[:, pix : 2 * pix]
    weight_ref[...] = total[:, 2 * pix :]


def finish(found, own, away):
    each, wide = own.shape
    return pl.pallas_call(
        finish_kernel,
        out_shape=[
            jax.ShapeDtypeStruct((each, 2, wide // 3), jnp.float32),
            jax.ShapeDtypeStruct((each, wide // 3), jnp.float32),
            jax.ShapeDtypeStruct(found.shape[1:], jnp.float32),
        ],
        compiler_params=pltpu.CompilerParams(vmem_limit_bytes=8 * 2**20),
        name="finish",
    )(found, own, *away)


def opening_kernel(out_ref):
    out_ref[...] = jnp.zeros_like(out_ref)


def opening():
    return pl.pallas_call(
        opening_kernel,
        out_specs=pl.BlockSpec(memory_space=pltpu.VMEM),
        out_shape=pltpu.VMEM((8, 128), jnp.float32),
        compiler_params=pltpu.CompilerParams(vmem_limit_bytes=2**20, has_side_effects=True),
        cost_estimate=pl.CostEstimate(flops=10**10, bytes_accessed=10**7, transcendentals=0),
        name="opening",
    )()


def entry(table, me):
    value = jnp.int32(table[0])
    for j in range(1, len(table)):
        value = jnp.where(me == j, jnp.int32(table[j]), value)
    return value


def swap(value, axes, size, mask):
    return lax.ppermute(value, axes, [(j ^ mask, j) for j in range(size)])


def body(images, ctf, projections, shifts, inv_sigma2, class_ids, log_prior, allowed):
    blocks = lax.axis_size("blk")
    pieces = lax.axis_size(("shell", "sub"))
    direct = blocks in FETCH

    first = opening()
    projections, first = lax.optimization_barrier((projections, first))
    if direct:
        projs = [projections] + [lax.ppermute(projections, "blk", [(source, j) for j, source in enumerate(sources)]) for sources in FETCH[blocks]]
    else:
        projs = [lax.all_gather(projections, "blk", axis=0, tiled=True)]
    data = prepare(images, ctf, shifts, inv_sigma2, pieces, first)
    part = score(data, allowed, class_ids, log_prior, projs, blocks, direct)
    if pieces == 4:
        parts = [part] + [swap(part, ("shell", "sub"), 4, mask) for mask in SHARE]
    else:
        parts = [lax.psum(part, ("shell", "sub"))]
    best, own, *away = back(data, parts, blocks - 1 if direct else 0, pieces)
    if not direct:
        own = lax.psum_scatter(own, "blk", scatter_dimension=0, tiled=True)
    arrived = [
        lax.ppermute(value, "blk", list(enumerate(goals))) for value, goals in zip(away, RETURN[blocks] if direct else ())
    ]
    return finish(best, own, arrived)


def solution(mesh):
    in_specs = (
        P(("groups", "blk"), None, ("shell", "sub")),
        P(("groups", "blk"), ("shell", "sub")),
        P(("groups", "blk"), None, ("shell", "sub")),
        P(("groups", "blk"), None),
        P(("shell", "sub")),
        P("groups"),
        P(),
        P(("groups", "blk"), None),
    )
    out_specs = (
        P(("groups", "blk"), None, ("shell", "sub")),
        P(("groups", "blk"), ("shell", "sub")),
        P(("groups", "blk", "shell", "sub")),
    )
    return jax.shard_map(body, mesh=mesh, in_specs=in_specs, out_specs=out_specs, check_vma=False)
```
